32 devices in a mesh: dp: 16 (over z, y, x), tensor: 2 (over core).
Axes of the slice: x: 2, y: 2, z: 4, core: 2. Of those that a mesh axis runs over, the one named last changes fastest.
Arguments:
- inputs: bfloat16 [2048, 4096], P(('dp', 'tensor')), may hold values from -6 to 6
- out_grad: bfloat16 [2048, 14336], P('dp', 'tensor'), may hold values from -6 to 6
- weight: bfloat16 [4096, 14336], P('dp', 'tensor'), may hold values from -0.09375 to 0.09375
- proj_basis: float32 [4096, 64], replicated, may hold values from -0.09375 to 0.09375
- momentum: float32 [4096, 14336], P('dp', 'tensor'), may hold values from -4 to 4
Outputs:
- input_grad: bfloat16 [2048, 4096], P(('dp', 'tensor'))
- new_momentum: float32 [4096, 14336], P('dp', 'tensor')
The draws below stay inside these ranges and needn't reach their ends.
All inputs are finite; a program needn't handle non-finite values.
Results may differ from the reference program's by a relative error of at most 0.017.
Values may be sent and summed in bfloat16 or wider, within the bound.
No kernel may reach another device: no remote copies, remote signals or barrier semaphores. Data moves between devices by JAX's collectives and lax.ppermute only.
A program may use at most 128 MiB of HBM per device.

```python
import math
import jax
import jax.numpy as jnp
from jax import lax

D = 4096
FF = 14336
RANK = 64
TOKENS = 2048
N_TENSOR = 2


def block_levels(own_key, extent, split, smallest, largest):
    gain = 1.0
    for dim, blocks in split:
        heights = jax.random.uniform(jax.random.fold_in(jax.random.fold_in(own_key, 6), dim), (blocks,), jnp.float32, smallest / len(split), largest / len(split))
        gain = gain * jnp.repeat(jnp.exp(heights), extent[dim] // blocks).reshape((-1,) + (1,) * (len(extent) - 1 - dim))
    return gain


def bell_draw(key, shape, spread, reach, shards=(), kind=jnp.bfloat16):
    values = spread * jax.random.normal(key, shape, jnp.float32)
    if shards:
        values = values * block_levels(key, shape, shards, -0.22, 0.18)
    return jnp.clip(values, -reach, reach).astype(kind)


def setup_inputs(seed: int = 0) -> dict:
    key_of = jax.random.split(jax.random.key(seed), 6)
    return {
        "inputs": bell_draw(key_of[0], (TOKENS, D), 1.0, 6.0, ((0, 32),)),
        "out_grad": bell_draw(key_of[1], (TOKENS, FF), 1.0, 6.0, ((0, 16), (1, 2))),
        "weight": bell_draw(key_of[2], (D, FF), D ** -0.5, 0.09375, ((0, 16), (1, 2))),
        "proj_basis": bell_draw(key_of[3], (D, RANK), D ** -0.5, 0.09375, (), jnp.float32),
        "momentum": bell_draw(key_of[4], (D, FF), 0.5, 4.0, ((0, 16), (1, 2)), jnp.float32),
    }


momentum_decay = 0.9

def reference(inputs, out_grad, weight, proj_basis, momentum):
    column_part = FF // N_TENSOR
    summed = jnp.zeros((TOKENS, D), jnp.float32)
    for block_index in range(N_TENSOR):
        grad_block = out_grad[:, block_index * column_part:(block_index + 1) * column_part]
        weight_block = weight[:, block_index * column_part:(block_index + 1) * column_part]
        partial_value = lax.dot_general(grad_block, weight_block, (((1,), (1,)), ((), ())), preferred_element_type=jnp.float32)
        rounded = lax.optimization_barrier(partial_value.astype(jnp.bfloat16))
        summed = summed + rounded.astype(jnp.float32)
    input_grad = summed.astype(jnp.bfloat16)
    projected = jnp.dot(inputs.astype(jnp.float32), proj_basis, precision=lax.Precision.HIGHEST).astype(jnp.bfloat16)
    grad_panel = lax.dot_general(projected, out_grad, (((0,), (0,)), ((), ())), preferred_element_type=jnp.float32)
    grad_panel = grad_panel / math.sqrt(TOKENS)
    update = jnp.dot(proj_basis, grad_panel, precision=lax.Precision.HIGHEST) * math.sqrt(D / RANK)
    new_momentum = momentum_decay * momentum + update
    return (input_grad, new_momentum)
```

```python
import math

import jax
import jax.numpy as jnp
from jax import lax
from jax.sharding import PartitionSpec as P

momentum_decay = 0.9
PLANE = 4
f32, bf16 = jnp.float32, jnp.bfloat16


def after(x, *first):
    return lax.optimization_barrier((x, first))[0]


def nt(a, b):
    return lax.dot_general(a, b, (((1,), (1,)), ((), ())), preferred_element_type=f32)


def tn(a, b):
    return lax.dot_general(a, b, (((0,), (0,)), ((), ())), preferred_element_type=f32)


class Layout:
    def __init__(self):
        self.replicas, self.cores = lax.axis_size("dp"), lax.axis_size("tensor")
        self.line = self.replicas // PLANE
        self.me, self.core = lax.axis_index("dp"), lax.axis_index("tensor")
        self.place, self.level = self.me % PLANE, self.me // PLANE

    def across(self, x, r):
        return lax.ppermute(x, "dp", [(d, d ^ r) for d in range(self.replicas)])

    def levels(self, x, s, only=None):
        pairs = [
            (d, d ^ (s * PLANE)) for d in range(self.replicas) if only is None or d // PLANE in only
        ]
        return lax.ppermute(x, "dp", pairs)

    def cut(self, x, r):
        quarter = x.shape[1] // PLANE
        return lax.dynamic_slice_in_dim(x, (self.place ^ r) * quarter, quarter, 1)

    def in_order(self, parts, axis):
        size = parts[0].shape[axis]
        shape = list(parts[0].shape)
        shape[axis] *= PLANE
        whole = jnp.zeros(shape, parts[0].dtype)
        for r, part in enumerate(parts):
            whole = lax.dynamic_update_slice_in_dim(whole, part, (self.place ^ r) * size, axis)
        return whole

    def core_sum(self, part, lines):
        width = part.shape[1]
        if self.cores == 2:
            part = part.reshape(lines, 2, -1, width)
            keep = lax.dynamic_index_in_dim(part, self.core, 1, False)
            give = lax.dynamic_index_in_dim(part, 1 - self.core, 1, False)
            got = lax.ppermute(give, "tensor", [(0, 1), (1, 0)])
            return (keep.astype(f32) + got.astype(f32)).astype(bf16)
        return lax.psum_scatter(
            part.reshape(lines, -1, width), "tensor", scatter_dimension=1, tiled=True
        )


def projected(lay, inputs, proj_basis):
    proj = jnp.dot(inputs.astype(f32), proj_basis, precision=lax.Precision.HIGHEST).astype(bf16)
    proj = lax.all_gather(proj, "tensor", axis=0, tiled=True)
    return [proj] + [lay.across(proj, r) for r in range(1, PLANE)]


def panel_shares(lay, plane_proj, pieces):
    panel = sum(tn(q, a) for q, a in zip(plane_proj, pieces))
    share = panel.shape[0] // lay.line
    share_of = lambda x, s: lax.dynamic_slice_in_dim(x, (lay.level ^ s) * share, share, 0)
    half = panel.astype(bf16)
    return [share_of(panel, 0)] + [lay.levels(share_of(half, s), s) for s in range(1, lay.line)]


def panel_quarter(lay, shares):
    summed = sum(x.astype(f32) for x in shares).astype(bf16)
    share, quarter = summed.shape
    panel_q = jnp.zeros((share * lay.line, quarter), bf16)
    for s in range(lay.line):
        got = lay.levels(summed, s) if s else summed
        panel_q = lax.dynamic_update_slice_in_dim(panel_q, got, (lay.level ^ s) * share, 0)
    return panel_q


def panel_whole(lay, panel_q):
    return lay.in_order([panel_q] + [lay.across(panel_q, r) for r in range(1, PLANE)], 1)


def updated(lay, proj_basis, panel, momentum, tokens):
    rows, rank = momentum.shape[0], proj_basis.shape[1]
    basis_rows = lax.dynamic_slice_in_dim(proj_basis, lay.me * rows, rows, 0)
    scale = math.sqrt(proj_basis.shape[0] / rank) / math.sqrt(tokens)
    update = jnp.dot(basis_rows.astype(bf16), panel, preferred_element_type=f32)
    return momentum_decay * momentum + update * scale


def long_line(inputs, out_grad, weight, proj_basis, momentum):
    lay = Layout()
    line, level, cores = lay.line, lay.level, lay.cores
    tokens = out_grad.shape[0]
    pieces = [lay.cut(out_grad, 0)] + [lay.across(lay.cut(out_grad, r), r) for r in range(1, PLANE)]
    weights = [lay.cut(weight, 0)] + [lay.across(lay.cut(weight, r), r) for r in range(1, PLANE)]
    groups = [[p + PLANE * z for z in range(line)] for p in range(PLANE)]
    shares = panel_shares(lay, projected(lay, inputs, proj_basis), pieces)
    panel = panel_whole(lay, panel_quarter(lay, shares))
    new_momentum = updated(lay, proj_basis, panel, momentum, tokens * lay.replicas)
    held = lay.in_order(weights, 0)
    width = held.shape[0]
    total = 0.0
    for r, piece in enumerate(pieces):
        block = lax.all_gather(piece, "dp", axis_index_groups=groups, axis=0, tiled=True)
        part = lay.core_sum(nt(block, held).astype(bf16), line)
        total = total + (lay.across(part, r) if r else part).astype(f32)
    total = total.astype(bf16)
    input_grad = jnp.zeros((tokens // cores, line * width), bf16)
    for s in range(line):
        got = lax.dynamic_index_in_dim(total, level ^ s, 0, False)
        got = lay.levels(got, s) if s else got
        input_grad = lax.dynamic_update_slice_in_dim(input_grad, got, (level ^ s) * width, 1)
    return input_grad, new_momentum


def line_of_four(inputs, out_grad, weight, proj_basis, momentum):
    lay = Layout()
    level, across = lay.level, lay.across
    inner = (level == 1) | (level == 2)
    tokens, hidden = out_grad.shape
    half = hidden // PLANE // 2
    end_swap = lambda x: lay.levels(x, 1)
    mid_swap = lambda x: lay.levels(x, 3, (1, 2))

    a0 = lay.cut(out_grad, 0)
    e0, m0 = end_swap(a0), mid_swap(a0)
    ax, ay = across(lay.cut(out_grad, 1), 1), across(lay.cut(out_grad, 2), 2)
    ad = across(after(lay.cut(out_grad, 3), ax, ay, e0, m0), 3)
    axy = jnp.concatenate([ax, ay], 0)
    axy = after(axy, e0, m0)
    e1, m1 = end_swap(axy), mid_swap(axy)
    plane_proj = projected(lay, after(inputs, a0), proj_basis)
    weight = after(weight, ax, ay)
    w1 = [lay.cut(weight, r)[:, half:] for r in range(PLANE)]
    w0 = [lay.cut(weight, r)[:, :half] for r in range(PLANE)]
    w1 = w1[:1] + [across(after(w1[r], ad), r) for r in range(1, PLANE)]
    shares = panel_shares(lay, plane_proj, [a0, ax, ay, ad])
    e2, m2 = end_swap(ad), mid_swap(ad)
    w0 = w0[:1] + [across(after(w0[r], *w1[1:]), r) for r in range(1, PLANE)]

    near_e, near_m = jnp.concatenate([e0, e1, e2], 0), jnp.concatenate([m0, m1, m2], 0)
    held1 = lay.in_order(w1, 0)
    cut_rows = held1.shape[0] // 2
    send = lambda a, w: jnp.where(inner, a, w)
    far0 = mid_swap(near_e[:, :half])
    got_a = end_swap(send(near_m[:, :half], held1[:cut_rows]))
    panel_q = panel_quarter(lay, shares)
    far1 = mid_swap(after(near_e[:, half:], far0))
    got_b = end_swap(send(far0, after(held1[cut_rows:], got_a)))
    panel = panel_whole(lay, after(panel_q, *w0[1:]))
    held0 = lay.in_order(w0, 0)
    held = jnp.concatenate([held0, held1], 1)
    width = held.shape[0]

    def plane_sum(part):
        part = lay.core_sum(part, PLANE)
        total = part[0].astype(f32)
        for r in range(1, PLANE):
            total = total + across(part[r], r).astype(f32)
        return total.astype(bf16)

    own = jnp.concatenate([a0, axy, ad], 0)
    y0, y1 = nt(own, held).astype(bf16), nt(near_e, held).astype(bf16)
    early = (nt(send(near_m[:, :half], got_a), held0) + nt(near_m[:, half:], held1)).astype(bf16)
    first = plane_sum(jnp.concatenate([y0, y1, early], 1))
    new_momentum = updated(lay, proj_basis, panel, momentum, tokens * lay.replicas)

    far1 = after(far1, new_momentum)
    late = (nt(send(far0, got_b), held0) + nt(far1, held1)).astype(bf16)
    other = jnp.concatenate([got_a, got_b], 0)
    early_other = nt(near_m[:, half:], other).astype(bf16)
    late_other = nt(far1, other).astype(bf16)
    second = plane_sum(after(jnp.concatenate([late, early_other, late_other], 1), first))
    y0, y1, early = [first[:, i * width:(i + 1) * width] for i in range(3)]
    late, early_other, late_other = [second[:, i * width:(i + 1) * width] for i in range(3)]

    z1 = end_swap(y1)
    z3 = mid_swap(early)
    z2 = lay.levels(early, 2, (0, 3))
    z2b = mid_swap(early_other)
    z_late = lay.levels(jnp.concatenate([late, late_other], 1), 2, (1, 2))
    z3b = lay.levels(late, 3, (0, 3))
    add = lambda *xs: sum(x.astype(f32) for x in xs).astype(bf16)
    z2 = add(z2, z2b, z_late[:, :width])
    z3 = add(z3, z3b, z_late[:, width:])
    by_distance = [y0, z1, z2, z3]
    input_grad = jnp.concatenate(
        [
            jnp.where(
                level == b,
                y0,
                jnp.where(level == b ^ 1, z1, jnp.where(level == b ^ 2, z2, z3)),
            )
            for b in range(len(by_distance))
        ],
        1,
    )
    return input_grad, new_momentum


def solution(mesh):
    placed = (
        P(("dp", "tensor"), None),
        P("dp", "tensor"),
        P("dp", "tensor"),
        P(),
        P("dp", "tensor"),
    )
    four = mesh.shape["dp"] == 4 * PLANE
    return jax.shard_map(
        line_of_four if four else long_line,
        mesh=mesh,
        in_specs=placed,
        out_specs=(P(("dp", "tensor"), None), P("dp", "tensor")),
        check_vma=False,
    )
```

```python
import math

import jax
import jax.numpy as jnp
from jax import lax
from jax.experimental import pallas as pl
from jax.experimental.pallas import tpu as pltpu
from jax.sharding import PartitionSpec as P

momentum_decay = 0.9
PLANE = 4
f32, bf16 = jnp.float32, jnp.bfloat16


def after(x, *first):
    return lax.optimization_barrier((x, first))[0]


def nt(a, b):
    return lax.dot_general(a, b, (((1,), (1,)), ((), ())), preferred_element_type=f32)


def tn(a, b):
    return lax.dot_general(a, b, (((0,), (0,)), ((), ())), preferred_element_type=f32)


class Layout:
    def __init__(self):
        self.replicas, self.cores = lax.axis_size("dp"), lax.axis_size("tensor")
        self.line = self.replicas // PLANE
        self.me, self.core = lax.axis_index("dp"), lax.axis_index("tensor")
        self.place, self.level = self.me % PLANE, self.me // PLANE

    def across(self, x, r):
        return lax.ppermute(x, "dp", [(d, d ^ r) for d in range(self.replicas)])

    def levels(self, x, s, only=None):
        pairs = [
            (d, d ^ (s * PLANE)) for d in range(self.replicas) if only is None or d // PLANE in only
        ]
        return lax.ppermute(x, "dp", pairs)

    def cut(self, x, r):
        quarter = x.shape[1] // PLANE
        return lax.dynamic_slice_in_dim(x, (self.place ^ r) * quarter, quarter, 1)

    def in_order(self, parts, axis):
        size = parts[0].shape[axis]
        shape = list(parts[0].shape)
        shape[axis] *= PLANE
        whole = jnp.zeros(shape, parts[0].dtype)
        for r, part in enumerate(parts):
            whole = lax.dynamic_update_slice_in_dim(whole, part, (self.place ^ r) * size, axis)
        return whole

    def core_sum(self, part, lines):
        width = part.shape[1]
        if self.cores == 2:
            part = part.reshape(lines, 2, -1, width)
            keep = lax.dynamic_index_in_dim(part, self.core, 1, False)
            give = lax.dynamic_index_in_dim(part, 1 - self.core, 1, False)
            got = lax.ppermute(give, "tensor", [(0, 1), (1, 0)])
            return (keep.astype(f32) + got.astype(f32)).astype(bf16)
        return lax.psum_scatter(
            part.reshape(lines, -1, width), "tensor", scatter_dimension=1, tiled=True
        )


def projected(lay, inputs, proj_basis):
    proj = jnp.dot(inputs.astype(f32), proj_basis, precision=lax.Precision.HIGHEST).astype(bf16)
    proj = lax.all_gather(proj, "tensor", axis=0, tiled=True)
    return [proj] + [lay.across(proj, r) for r in range(1, PLANE)]


def panel_shares(lay, plane_proj, pieces):
    panel = sum(tn(q, a) for q, a in zip(plane_proj, pieces))
    share = panel.shape[0] // lay.line
    share_of = lambda x, s: lax.dynamic_slice_in_dim(x, (lay.level ^ s) * share, share, 0)
    half = panel.astype(bf16)
    return [share_of(panel, 0)] + [lay.levels(share_of(half, s), s) for s in range(1, lay.line)]


def panel_quarter(lay, shares):
    summed = sum(x.astype(f32) for x in shares).astype(bf16)
    share, quarter = summed.shape
    panel_q = jnp.zeros((share * lay.line, quarter), bf16)
    for s in range(lay.line):
        got = lay.levels(summed, s) if s else summed
        panel_q = lax.dynamic_update_slice_in_dim(panel_q, got, (lay.level ^ s) * share, 0)
    return panel_q


def panel_whole(lay, panel_q):
    return lay.in_order([panel_q] + [lay.across(panel_q, r) for r in range(1, PLANE)], 1)


def updated(lay, proj_basis, panel, momentum, tokens):
    rows, rank = momentum.shape[0], proj_basis.shape[1]
    basis_rows = lax.dynamic_slice_in_dim(proj_basis, lay.me * rows, rows, 0)
    scale = math.sqrt(proj_basis.shape[0] / rank) / math.sqrt(tokens)
    update = jnp.dot(basis_rows.astype(bf16), panel, preferred_element_type=f32)
    return momentum_decay * momentum + update * scale


def long_line(inputs, out_grad, weight, proj_basis, momentum):
    lay = Layout()
    line, level, cores = lay.line, lay.level, lay.cores
    tokens = out_grad.shape[0]
    pieces = [lay.cut(out_grad, 0)] + [lay.across(lay.cut(out_grad, r), r) for r in range(1, PLANE)]
    weights = [lay.cut(weight, 0)] + [lay.across(lay.cut(weight, r), r) for r in range(1, PLANE)]
    groups = [[p + PLANE * z for z in range(line)] for p in range(PLANE)]
    shares = panel_shares(lay, projected(lay, inputs, proj_basis), pieces)
    panel = panel_whole(lay, panel_quarter(lay, shares))
    new_momentum = updated(lay, proj_basis, panel, momentum, tokens * lay.replicas)
    held = lay.in_order(weights, 0)
    width = held.shape[0]
    total = 0.0
    for r, piece in enumerate(pieces):
        block = lax.all_gather(piece, "dp", axis_index_groups=groups, axis=0, tiled=True)
        part = lay.core_sum(nt(block, held).astype(bf16), line)
        total = total + (lay.across(part, r) if r else part).astype(f32)
    total = total.astype(bf16)
    input_grad = jnp.zeros((tokens // cores, line * width), bf16)
    for s in range(line):
        got = lax.dynamic_index_in_dim(total, level ^ s, 0, False)
        got = lay.levels(got, s) if s else got
        input_grad = lax.dynamic_update_slice_in_dim(input_grad, got, (level ^ s) * width, 1)
    return input_grad, new_momentum


def products(lay, sources, buffers, fills, jobs, width):
    scalars = jnp.stack([lay.place, lay.core]).astype(jnp.int32)
    rows = buffers[jobs[0][0]][0]
    half = rows // PLANE // 2
    piece = width // PLANE

    def kernel(scalar_ref, *refs):
        ins, refs = refs[: len(sources)], refs[len(sources):]
        keep_ref, give_ref, *scratch = refs
        buffer_refs, sems = scratch[:-1], scratch[-1]
        place, core = scalar_ref[0], scalar_ref[1]
        copies = []
        for i, (s, c0, b, r0, c1, cols) in enumerate(fills):
            n = sources[s].shape[0]
            copies.append(
                pltpu.make_async_copy(
                    ins[s].at[:, pl.ds(c0, cols)],
                    buffer_refs[b].at[pl.ds(r0, n), pl.ds(c1, cols)],
                    sems.at[i],
                )
            )
        for copy in copies:
            copy.start()
        waited = set()

        def need(ids):
            for i in ids:
                if i not in waited:
                    copies[i].wait()
                    waited.add(i)

        for at, (a, b, a0, b0, cols, a_ids, b_ids) in enumerate(jobs):
            need(a_ids)
            for r in range(PLANE):
                need(b_ids(r))
                x = nt(
                    buffer_refs[a][:, a0:a0 + cols],
                    buffer_refs[b][r * piece:(r + 1) * piece, b0:b0 + cols],
                ).astype(bf16)
                column = at * width + pl.multiple_of((place ^ r) * piece, piece)
                for p in range(PLANE):
                    low = x[2 * p * half:(2 * p + 1) * half]
                    high = x[(2 * p + 1) * half:(2 * p + 2) * half]
                    keep_ref[p, :, pl.ds(column, piece)] = jnp.where(core == 0, low, high)
                    give_ref[p, :, pl.ds(column, piece)] = jnp.where(core == 0, high, low)
        need(range(len(copies)))

    out = jax.ShapeDtypeStruct((PLANE, half, len(jobs) * width), bf16)
    return pl.pallas_call(
        kernel,
        out_shape=(out, out),
        in_specs=[pl.BlockSpec(memory_space=pltpu.SMEM)]
        + [pl.BlockSpec(memory_space=pl.ANY)] * len(sources),
        out_specs=[pl.BlockSpec(memory_space=pltpu.VMEM)] * 2,
        scratch_shapes=[pltpu.VMEM(shape, bf16) for shape in buffers]
        + [pltpu.SemaphoreType.DMA((len(fills),))],
        compiler_params=pltpu.CompilerParams(vmem_limit_bytes=36 * 2**20),
        cost_estimate=pl.CostEstimate(flops=10**6, bytes_accessed=10**5, transcendentals=0),
    )(scalars, *sources)


def line_of_four(inputs, out_grad, weight, proj_basis, momentum):
    lay = Layout()
    level, across = lay.level, lay.across
    inner = (level == 1) | (level == 2)
    tokens, hidden = out_grad.shape
    rows = weight.shape[0]
    width = rows * PLANE
    half = hidden // PLANE // 2
    end_swap = lambda x: lay.levels(x, 1)
    mid_swap = lambda x: lay.levels(x, 3, (1, 2))
    outward = lambda x: lay.levels(x, 1, (1, 2))
    inward = lambda x: lay.levels(x, 1, (0, 3))
    send = lambda a, w: jnp.where(inner, a, w)
    end_sent, mid_sent = [], []

    def queued(move, sent, x, *first):
        got = move(after(x, *sent[-2:-1], *first))
        sent.append(got)
        return got

    a0 = lay.cut(out_grad, 0)
    e0, m0 = queued(end_swap, end_sent, a0), queued(mid_swap, mid_sent, a0)
    cuts = [lay.cut(after(out_grad, a0), r) for r in range(1, PLANE)]
    ax, ay = across(cuts[0], 1), across(cuts[1], 2)
    ad = across(after(cuts[2], ax, ay, e0, m0), 3)
    axy = after(jnp.concatenate([ax, ay], 0), e0, m0)
    e1, m1 = queued(end_swap, end_sent, axy), queued(mid_swap, mid_sent, axy)
    proj = projected(lay, after(inputs, *cuts), proj_basis)
    weight = after(weight, ax, ay)
    parts = [lay.cut(weight, r) for r in range(PLANE)]
    parts[1:3] = [across(after(parts[r], ad), r) for r in (1, 2)]
    parts[3] = across(after(parts[3], parts[1], parts[2]), 3)
    e2, m2 = queued(end_swap, end_sent, ad), queued(mid_swap, mid_sent, ad)

    panel = sum(tn(q, a) for q, a in zip(proj, [a0, ax, ay, ad]))
    panel = panel + inward(after(panel.astype(bf16), e1, m1)).astype(f32)

    near_e, near_m = jnp.concatenate([e0, e1, e2], 0), jnp.concatenate([m0, m1, m2], 0)
    pair = 2 * tokens
    far0, far1, got = [], [], []
    for i in range(2):
        far0.append(queued(mid_swap, mid_sent, near_e[i * pair:(i + 1) * pair, :half]))
        got.append(queued(end_swap, end_sent, send(near_m[i * pair:(i + 1) * pair, :half], parts[i][:, half:])))
    pair_panel = panel
    other_pair = mid_swap(after(panel.astype(bf16), far0[0], got[0]))
    for i in range(2):
        far1.append(queued(mid_swap, mid_sent, near_e[i * pair:(i + 1) * pair, half:]))
        got.append(queued(end_swap, end_sent, send(far0[i], parts[2 + i][:, half:]), parts[3]))
    def weight_fills(first, buffer):
        return [(first + r, 0, buffer, r * rows, 0, 2 * half) for r in range(PLANE)]

    def block_fills(first, buffer, sizes, column, cols):
        out, row = [], 0
        for i, n in enumerate(sizes):
            out.append((first + i, column, buffer, row, column, cols))
            row += n
        return out

    both = 2 * half
    early0 = send(near_m[:, :half], jnp.concatenate(got[:2], 0))
    sources = [after(a0, *far0, pair_panel), ax, ay, ad, *parts, near_e, early0, near_m]
    fills = block_fills(0, 0, [tokens] * PLANE, 0, both) + weight_fills(4, 3)
    fills += [(8, 0, 1, 0, 0, both), (9, 0, 2, 0, 0, half), (10, half, 2, 0, half, half)]
    wide, tall = (PLANE * tokens, both), (width, both)
    of_weight = lambda r: (4 + r,)
    none = lambda r: ()
    jobs = [
        (0, 3, 0, 0, both, range(4), of_weight),
        (1, 3, 0, 0, both, (8,), none),
        (2, 3, 0, 0, both, (9, 10), none),
    ]
    keep, give = products(lay, sources, [wide, wide, wide, tall], fills, jobs, width)
    swap = lambda x: lax.ppermute(x, "tensor", [(0, 1), (1, 0)])
    give = after(give, far1[0], got[2])
    panel = (panel + after(other_pair, keep).astype(f32)).astype(bf16)
    panel = send(panel, outward(after(panel, far1[0], got[2])))
    first = (keep.astype(f32) + swap(give).astype(f32)).astype(bf16)

    late0 = [send(far0[i], got[2 + i]) for i in range(2)]
    late0[0] = after(late0[0], first)
    sources = [*late0, *far1, near_m, *parts, *got]
    fills = [(i, 0, 0, i * pair, 0, half) for i in range(2)]
    fills += [(2 + i, 0, 0, i * pair, half, half) for i in range(2)]
    fills += weight_fills(5, 2) + [(4, half, 1, 0, 0, half)]
    fills += [(9 + r, 0, 3, r * rows, 0, half) for r in range(PLANE)]
    jobs = [
        (0, 2, 0, 0, both, range(4), of_weight),
        (1, 3, 0, 0, half, (8,), lambda r: (9 + r,)),
        (0, 3, half, 0, half, (), none),
    ]
    buffers = [wide, (PLANE * tokens, half), tall, (width, half)]
    keep, give = products(lay, sources, buffers, fills, jobs, width)

    def plane_sum(part):
        total = part[0].astype(f32)
        for r in range(1, PLANE):
            total = total + across(part[r], r).astype(f32)
        return total.astype(bf16)

    first = plane_sum(first)
    second = (keep.astype(f32) + swap(after(give, first, panel)).astype(f32)).astype(bf16)
    panel = after(panel, second)
    panel = lay.in_order([panel] + [across(panel, r) for r in range(1, PLANE)], 1)
    new_momentum = updated(lay, proj_basis, panel, momentum, tokens * lay.replicas)
    second = plane_sum(second)
    y0, y1, early = [first[:, i * width:(i + 1) * width] for i in range(3)]
    late, early_other, late_other = [second[:, i * width:(i + 1) * width] for i in range(3)]

    z1 = end_swap(y1)
    z3 = mid_swap(early)
    z2 = lay.levels(early, 2, (0, 3))
    z2b = mid_swap(early_other)
    z_late = lay.levels(jnp.concatenate([late, late_other], 1), 2, (1, 2))
    z3b = lay.levels(late, 3, (0, 3))
    add = lambda *xs: sum(x.astype(f32) for x in xs).astype(bf16)
    z2 = add(z2, z2b, z_late[:, :width])
    z3 = add(z3, z3b, z_late[:, width:])
    input_grad = jnp.concatenate(
        [
            jnp.where(
                level == b,
                y0,
                jnp.where(level == b ^ 1, z1, jnp.where(level == b ^ 2, z2, z3)),
            )
            for b in range(lay.line)
        ],
        1,
    )
    return input_grad, new_momentum


def solution(mesh):
    placed = (
        P(("dp", "tensor"), None),
        P("dp", "tensor"),
        P("dp", "tensor"),
        P(),
        P("dp", "tensor"),
    )
    four = mesh.shape["dp"] == 4 * PLANE and mesh.shape["tensor"] == 2
    return jax.shard_map(
        line_of_four if four else long_line,
        mesh=mesh,
        in_specs=placed,
        out_specs=(P(("dp", "tensor"), None), P("dp", "tensor")),
        check_vma=False,
    )
```

```python
import math

import jax
import jax.numpy as jnp
from jax import lax
from jax.experimental import pallas as pl
from jax.experimental.pallas import tpu as pltpu
from jax.sharding import PartitionSpec as P

momentum_decay = 0.9
PLANE = 4
f32, bf16 = jnp.float32, jnp.bfloat16


def after(x, *first):
    return lax.optimization_barrier((x, first))[0]


def nt(a, b):
    return lax.dot_general(a, b, (((1,), (1,)), ((), ())), preferred_element_type=f32)


def tn(a, b):
    return lax.dot_general(a, b, (((0,), (0,)), ((), ())), preferred_element_type=f32)


class Layout:
    def __init__(self):
        self.replicas, self.cores = lax.axis_size("dp"), lax.axis_size("tensor")
        self.line = self.replicas // PLANE
        self.me, self.core = lax.axis_index("dp"), lax.axis_index("tensor")
        self.place, self.level = self.me % PLANE, self.me // PLANE

    def across(self, x, r):
        return lax.ppermute(x, "dp", [(d, d ^ r) for d in range(self.replicas)])

    def levels(self, x, s, only=None):
        pairs = [
            (d, d ^ (s * PLANE)) for d in range(self.replicas) if only is None or d // PLANE in only
        ]
        return lax.ppermute(x, "dp", pairs)

    def cut(self, x, r):
        quarter = x.shape[1] // PLANE
        return lax.dynamic_slice_in_dim(x, (self.place ^ r) * quarter, quarter, 1)

    def in_order(self, parts, axis):
        size = parts[0].shape[axis]
        shape = list(parts[0].shape)
        shape[axis] *= PLANE
        whole = jnp.zeros(shape, parts[0].dtype)
        for r, part in enumerate(parts):
            whole = lax.dynamic_update_slice_in_dim(whole, part, (self.place ^ r) * size, axis)
        return whole

    def core_sum(self, part, lines):
        width = part.shape[1]
        if self.cores == 2:
            part = part.reshape(lines, 2, -1, width)
            keep = lax.dynamic_index_in_dim(part, self.core, 1, False)
            give = lax.dynamic_index_in_dim(part, 1 - self.core, 1, False)
            got = lax.ppermute(give, "tensor", [(0, 1), (1, 0)])
            return (keep.astype(f32) + got.astype(f32)).astype(bf16)
        return lax.psum_scatter(
            part.reshape(lines, -1, width), "tensor", scatter_dimension=1, tiled=True
        )


def projected(lay, inputs, proj_basis):
    proj = jnp.dot(inputs.astype(f32), proj_basis, precision=lax.Precision.HIGHEST).astype(bf16)
    proj = lax.all_gather(proj, "tensor", axis=0, tiled=True)
    return [proj] + [lay.across(proj, r) for r in range(1, PLANE)]


def panel_shares(lay, plane_proj, pieces):
    panel = sum(tn(q, a) for q, a in zip(plane_proj, pieces))
    share = panel.shape[0] // lay.line
    share_of = lambda x, s: lax.dynamic_slice_in_dim(x, (lay.level ^ s) * share, share, 0)
    half = panel.astype(bf16)
    return [share_of(panel, 0)] + [lay.levels(share_of(half, s), s) for s in range(1, lay.line)]


def panel_quarter(lay, shares):
    summed = sum(x.astype(f32) for x in shares).astype(bf16)
    share, quarter = summed.shape
    panel_q = jnp.zeros((share * lay.line, quarter), bf16)
    for s in range(lay.line):
        got = lay.levels(summed, s) if s else summed
        panel_q = lax.dynamic_update_slice_in_dim(panel_q, got, (lay.level ^ s) * share, 0)
    return panel_q


def panel_whole(lay, panel_q):
    return lay.in_order([panel_q] + [lay.across(panel_q, r) for r in range(1, PLANE)], 1)


def updated(lay, proj_basis, panel, momentum, tokens):
    rows, rank = momentum.shape[0], proj_basis.shape[1]
    basis_rows = lax.dynamic_slice_in_dim(proj_basis, lay.me * rows, rows, 0)
    scale = math.sqrt(proj_basis.shape[0] / rank) / math.sqrt(tokens)
    update = jnp.dot(basis_rows.astype(bf16), panel, preferred_element_type=f32)
    return momentum_decay * momentum + update * scale


def long_line(inputs, out_grad, weight, proj_basis, momentum):
    lay = Layout()
    line, level, cores = lay.line, lay.level, lay.cores
    tokens = out_grad.shape[0]
    pieces = [lay.cut(out_grad, 0)] + [lay.across(lay.cut(out_grad, r), r) for r in range(1, PLANE)]
    weights = [lay.cut(weight, 0)] + [lay.across(lay.cut(weight, r), r) for r in range(1, PLANE)]
    groups = [[p + PLANE * z for z in range(line)] for p in range(PLANE)]
    shares = panel_shares(lay, projected(lay, inputs, proj_basis), pieces)
    panel = panel_whole(lay, panel_quarter(lay, shares))
    new_momentum = updated(lay, proj_basis, panel, momentum, tokens * lay.replicas)
    held = lay.in_order(weights, 0)
    width = held.shape[0]
    total = 0.0
    for r, piece in enumerate(pieces):
        block = lax.all_gather(piece, "dp", axis_index_groups=groups, axis=0, tiled=True)
        part = lay.core_sum(nt(block, held).astype(bf16), line)
        total = total + (lay.across(part, r) if r else part).astype(f32)
    total = total.astype(bf16)
    input_grad = jnp.zeros((tokens // cores, line * width), bf16)
    for s in range(line):
        got = lax.dynamic_index_in_dim(total, level ^ s, 0, False)
        got = lay.levels(got, s) if s else got
        input_grad = lax.dynamic_update_slice_in_dim(input_grad, got, (level ^ s) * width, 1)
    return input_grad, new_momentum


def products(lay, sources, buffers, fills, jobs, width, blocks):
    scalars = jnp.stack([lay.place, lay.core]).astype(jnp.int32)
    piece = width // PLANE
    block = sum(job[2] for job in jobs) // blocks
    half = block // PLANE // 2

    def kernel(scalar_ref, *refs):
        ins, refs = refs[: len(sources)], refs[len(sources):]
        keep_ref, give_ref, *scratch = refs
        buffer_refs, sems = scratch[:-1], scratch[-1]
        place, core = scalar_ref[0], scalar_ref[1]
        copies = []
        for i, (s, c0, b, r0, c1, cols) in enumerate(fills):
            n = sources[s].shape[0]
            copies.append(
                pltpu.make_async_copy(
                    ins[s].at[:, pl.ds(c0, cols)],
                    buffer_refs[b].at[pl.ds(r0, n), pl.ds(c1, cols)],
                    sems.at[i],
                )
            )
        for copy in copies:
            copy.start()
        waited = set()

        def need(ids):
            for i in ids:
                if i not in waited:
                    copies[i].wait()
                    waited.add(i)

        for a, row, count, a0, b, b0, cols, a_ids, b_ids, first in jobs:
            need(a_ids)
            for r in range(PLANE):
                need(b_ids(r))
                x = nt(
                    buffer_refs[a][row:row + count, a0:a0 + cols],
                    buffer_refs[b][r * piece:(r + 1) * piece, b0:b0 + cols],
                ).astype(bf16)
                for at in range(count // block):
                    column = (first + at) * width + pl.multiple_of((place ^ r) * piece, piece)
                    for p in range(PLANE):
                        low = x[at * block + 2 * p * half:][:half]
                        high = x[at * block + (2 * p + 1) * half:][:half]
                        keep_ref[p, :, pl.ds(column, piece)] = jnp.where(core == 0, low, high)
                        give_ref[p, :, pl.ds(column, piece)] = jnp.where(core == 0, high, low)
        need(range(len(copies)))

    out = jax.ShapeDtypeStruct((PLANE, half, blocks * width), bf16)
    return pl.pallas_call(
        kernel,
        out_shape=(out, out),
        in_specs=[pl.BlockSpec(memory_space=pltpu.SMEM)]
        + [pl.BlockSpec(memory_space=pl.ANY)] * len(sources),
        out_specs=[pl.BlockSpec(memory_space=pltpu.VMEM)] * 2,
        scratch_shapes=[pltpu.VMEM(shape, bf16) for shape in buffers]
        + [pltpu.SemaphoreType.DMA((len(fills),))],
        compiler_params=pltpu.CompilerParams(vmem_limit_bytes=36 * 2**20),
        cost_estimate=pl.CostEstimate(flops=10**6, bytes_accessed=10**5, transcendentals=0),
    )(scalars, *sources)


def line_of_four(inputs, out_grad, weight, proj_basis, momentum):
    lay = Layout()
    level, across = lay.level, lay.across
    inner = (level == 1) | (level == 2)
    tokens, hidden = out_grad.shape
    rows = weight.shape[0]
    width = rows * PLANE
    half = hidden // PLANE // 2
    end_swap = lambda x: lay.levels(x, 1)
    mid_swap = lambda x: lay.levels(x, 3, (1, 2))
    outward = lambda x: lay.levels(x, 1, (1, 2))
    inward = lambda x: lay.levels(x, 1, (0, 3))
    send = lambda a, w: jnp.where(inner, a, w)
    end_sent, mid_sent = [], []

    def queued(move, sent, x, *first):
        got = move(after(x, *sent[-2:-1], *first))
        sent.append(got)
        return got

    cuts = [lay.cut(out_grad, r) for r in range(PLANE)]
    ax, ay = across(cuts[1], 1), across(cuts[2], 2)
    e0, m0 = queued(end_swap, end_sent, cuts[0]), queued(mid_swap, mid_sent, cuts[0])
    proj = projected(lay, after(inputs, *cuts), proj_basis)
    weight = after(weight, proj[0])
    parts = [lay.cut(weight, r) for r in range(PLANE)]
    ad = across(after(cuts[3], proj[0], ax, ay), 3)
    e1, m1 = queued(end_swap, end_sent, ax), queued(mid_swap, mid_sent, ax)
    parts[1:3] = [across(after(parts[r], ax, ay), r) for r in (1, 2)]
    ayd = jnp.concatenate([ay, ad], 0)
    e2, m2 = queued(end_swap, end_sent, ayd), queued(mid_swap, mid_sent, ayd)
    parts[3] = across(after(parts[3], ad, parts[1]), 3)
    own, near_e, near_m = [cuts[0], ax, ayd], [e0, e1, e2], [m0, m1, m2]
    halves = lambda x, c: [jnp.concatenate([x[0][:, c], x[1][:, c]], 0), x[2][:, c]]
    low, high = slice(0, half), slice(half, 2 * half)

    panel = sum(tn(q, a) for q, a in zip(proj, [cuts[0], ax, ay, ad]))
    panel = panel + inward(after(panel.astype(bf16), e1, m1)).astype(f32)

    far0, far1, got = [], [], []
    for x, m, w in zip(halves(near_e, low), halves(near_m, low), parts):
        far0.append(queued(mid_swap, mid_sent, x))
        got.append(queued(end_swap, end_sent, send(m, w[:, high])))
    other_pair = mid_swap(after(panel.astype(bf16), far0[0]))
    for x, f, w in zip(halves(near_e, high), far0, parts[2:]):
        far1.append(queued(mid_swap, mid_sent, x))
        got.append(queued(end_swap, end_sent, send(f, w[:, high]), parts[3]))

    def weight_fills(first, buffer):
        return [(first + r, 0, buffer, r * rows, 0, 2 * half) for r in range(PLANE)]

    def block_fills(first, buffer, sizes, column, row, cols):
        out = []
        for i, n in enumerate(sizes):
            out.append((first + i, column, buffer, row, column, cols))
            row += n
        return out

    both = 2 * half
    sizes = [tokens, tokens, 2 * tokens]
    block = PLANE * tokens
    early0 = jnp.concatenate([send(m, g) for m, g in zip(halves(near_m, low), got)], 0)
    sources = [*own, *near_e, *near_m, early0, *parts]
    sources[0] = after(sources[0], *far0, panel)
    fills = block_fills(0, 0, sizes, 0, 0, both)
    fills += weight_fills(10, 1)
    fills += block_fills(3, 0, sizes, 0, block, both) + [(9, 0, 0, 2 * block, 0, half)]
    fills += block_fills(6, 0, sizes, half, 2 * block, half)
    of_weight = lambda r: (3 + r,)
    none = lambda r: ()
    jobs = [(0, 0, 3 * block, 0, 1, 0, both, (*range(3), *range(7, 14)), of_weight, 0)]
    buffers = [(3 * block, both), (width, both)]
    keep, give = products(lay, sources, buffers, fills, jobs, width, 3)
    swap = lambda x: lax.ppermute(x, "tensor", [(0, 1), (1, 0)])
    give = after(give, far1[0], got[2])
    first = (keep.astype(f32) + swap(give).astype(f32)).astype(bf16)
    panel = (panel + after(other_pair, first).astype(f32)).astype(bf16)
    panel = send(panel, outward(after(panel, far1[0], got[2])))

    late0 = [send(far0[i], got[2 + i]) for i in range(2)]
    sources = [*late0, *far1, *near_m, *parts, *got]
    sources[0] = after(sources[0], first)
    pair = 2 * tokens
    fills = [(i, 0, 0, i * pair, 0, half) for i in range(2)]
    fills += [(2 + i, 0, 0, i * pair, half, half) for i in range(2)]
    fills += weight_fills(7, 2)
    fills += [(s, c, b, r0, 0, n) for s, c, b, r0, _, n in block_fills(4, 1, sizes, half, 0, half)]
    fills += [(2 + i, 0, 1, block + i * pair, 0, half) for i in range(2)]
    fills += [(11 + r, 0, 3, r * rows, 0, half) for r in range(PLANE)]
    of_weight = lambda r: (4 + r,)
    jobs = [
        (0, 0, block, 0, 2, 0, both, range(4), of_weight, 0),
        (1, 0, 2 * block, 0, 3, 0, half, range(8, 13), lambda r: (13 + r,), 1),
    ]
    buffers = [(block, both), (2 * block, half), (width, both), (width, half)]
    keep, give = products(lay, sources, buffers, fills, jobs, width, 3)

    def plane_sum(part):
        total = part[0].astype(f32)
        for r in range(1, PLANE):
            total = total + across(part[r], r).astype(f32)
        return total.astype(bf16)

    first = plane_sum(first)
    second = (keep.astype(f32) + swap(after(give, first, panel)).astype(f32)).astype(bf16)
    second = plane_sum(second)
    panel = after(panel, second)
    panel = lay.in_order([panel] + [across(panel, r) for r in range(1, PLANE)], 1)
    new_momentum = updated(lay, proj_basis, panel, momentum, tokens * lay.replicas)
    y0, y1, early = [first[:, i * width:(i + 1) * width] for i in range(3)]
    late, early_other, late_other = [second[:, i * width:(i + 1) * width] for i in range(3)]

    z1 = end_swap(y1)
    z3 = mid_swap(early)
    z2 = lay.levels(early, 2, (0, 3))
    z2b = mid_swap(early_other)
    z_late = lay.levels(jnp.concatenate([late, late_other], 1), 2, (1, 2))
    z3b = lay.levels(late, 3, (0, 3))
    add = lambda *xs: sum(x.astype(f32) for x in xs).astype(bf16)
    z2 = add(z2, z2b, z_late[:, :width])
    z3 = add(z3, z3b, z_late[:, width:])
    input_grad = jnp.concatenate(
        [
            jnp.where(
                level == b,
                y0,
                jnp.where(level == b ^ 1, z1, jnp.where(level == b ^ 2, z2, z3)),
            )
            for b in range(lay.line)
        ],
        1,
    )
    return input_grad, new_momentum


def solution(mesh):
    placed = (
        P(("dp", "tensor"), None),
        P("dp", "tensor"),
        P("dp", "tensor"),
        P(),
        P("dp", "tensor"),
    )
    four = mesh.shape["dp"] == 4 * PLANE and mesh.shape["tensor"] == 2
    return jax.shard_map(
        line_of_four if four else long_line,
        mesh=mesh,
        in_specs=placed,
        out_specs=(P(("dp", "tensor"), None), P("dp", "tensor")),
        check_vma=False,
    )
```

```python
import math

import jax
import jax.numpy as jnp
from jax import lax
from jax.experimental import pallas as pl
from jax.experimental.pallas import tpu as pltpu
from jax.sharding import PartitionSpec as P

momentum_decay = 0.9
PLANE = 4
f32, bf16 = jnp.float32, jnp.bfloat16


def after(x, *first):
    return lax.optimization_barrier((x, first))[0]


def nt(a, b):
    return lax.dot_general(a, b, (((1,), (1,)), ((), ())), preferred_element_type=f32)


def tn(a, b):
    return lax.dot_general(a, b, (((0,), (0,)), ((), ())), preferred_element_type=f32)


class Layout:
    def __init__(self):
        self.replicas, self.cores = lax.axis_size("dp"), lax.axis_size("tensor")
        self.line = self.replicas // PLANE
        self.me, self.core = lax.axis_index("dp"), lax.axis_index("tensor")
        self.place, self.level = self.me % PLANE, self.me // PLANE

    def across(self, x, r):
        return lax.ppermute(x, "dp", [(d, d ^ r) for d in range(self.replicas)])

    def levels(self, x, s, only=None):
        pairs = [
            (d, d ^ (s * PLANE)) for d in range(self.replicas) if only is None or d // PLANE in only
        ]
        return lax.ppermute(x, "dp", pairs)

    def cut(self, x, r):
        quarter = x.shape[1] // PLANE
        return lax.dynamic_slice_in_dim(x, (self.place ^ r) * quarter, quarter, 1)

    def in_order(self, parts, axis):
        size = parts[0].shape[axis]
        shape = list(parts[0].shape)
        shape[axis] *= PLANE
        whole = jnp.zeros(shape, parts[0].dtype)
        for r, part in enumerate(parts):
            whole = lax.dynamic_update_slice_in_dim(whole, part, (self.place ^ r) * size, axis)
        return whole

    def core_sum(self, part, lines):
        width = part.shape[1]
        if self.cores == 2:
            part = part.reshape(lines, 2, -1, width)
            keep = lax.dynamic_index_in_dim(part, self.core, 1, False)
            give = lax.dynamic_index_in_dim(part, 1 - self.core, 1, False)
            got = lax.ppermute(give, "tensor", [(0, 1), (1, 0)])
            return (keep.astype(f32) + got.astype(f32)).astype(bf16)
        return lax.psum_scatter(
            part.reshape(lines, -1, width), "tensor", scatter_dimension=1, tiled=True
        )


def projected(lay, inputs, proj_basis):
    proj = jnp.dot(inputs.astype(f32), proj_basis, precision=lax.Precision.HIGHEST).astype(bf16)
    proj = lax.all_gather(proj, "tensor", axis=0, tiled=True)
    return [proj] + [lay.across(proj, r) for r in range(1, PLANE)]


def panel_shares(lay, plane_proj, pieces):
    panel = sum(tn(q, a) for q, a in zip(plane_proj, pieces))
    share = panel.shape[0] // lay.line
    share_of = lambda x, s: lax.dynamic_slice_in_dim(x, (lay.level ^ s) * share, share, 0)
    half = panel.astype(bf16)
    return [share_of(panel, 0)] + [lay.levels(share_of(half, s), s) for s in range(1, lay.line)]


def panel_quarter(lay, shares):
    summed = sum(x.astype(f32) for x in shares).astype(bf16)
    share, quarter = summed.shape
    panel_q = jnp.zeros((share * lay.line, quarter), bf16)
    for s in range(lay.line):
        got = lay.levels(summed, s) if s else summed
        panel_q = lax.dynamic_update_slice_in_dim(panel_q, got, (lay.level ^ s) * share, 0)
    return panel_q


def panel_whole(lay, panel_q):
    return lay.in_order([panel_q] + [lay.across(panel_q, r) for r in range(1, PLANE)], 1)


def updated(lay, proj_basis, panel, momentum, tokens):
    rows, rank = momentum.shape[0], proj_basis.shape[1]
    basis_rows = lax.dynamic_slice_in_dim(proj_basis, lay.me * rows, rows, 0)
    scale = math.sqrt(proj_basis.shape[0] / rank) / math.sqrt(tokens)
    update = jnp.dot(basis_rows.astype(bf16), panel, preferred_element_type=f32)
    return momentum_decay * momentum + update * scale


def long_line(inputs, out_grad, weight, proj_basis, momentum):
    lay = Layout()
    line, level, cores = lay.line, lay.level, lay.cores
    tokens = out_grad.shape[0]
    pieces = [lay.cut(out_grad, 0)] + [lay.across(lay.cut(out_grad, r), r) for r in range(1, PLANE)]
    weights = [lay.cut(weight, 0)] + [lay.across(lay.cut(weight, r), r) for r in range(1, PLANE)]
    groups = [[p + PLANE * z for z in range(line)] for p in range(PLANE)]
    shares = panel_shares(lay, projected(lay, inputs, proj_basis), pieces)
    panel = panel_whole(lay, panel_quarter(lay, shares))
    new_momentum = updated(lay, proj_basis, panel, momentum, tokens * lay.replicas)
    held = lay.in_order(weights, 0)
    width = held.shape[0]
    total = 0.0
    for r, piece in enumerate(pieces):
        block = lax.all_gather(piece, "dp", axis_index_groups=groups, axis=0, tiled=True)
        part = lay.core_sum(nt(block, held).astype(bf16), line)
        total = total + (lay.across(part, r) if r else part).astype(f32)
    total = total.astype(bf16)
    input_grad = jnp.zeros((tokens // cores, line * width), bf16)
    for s in range(line):
        got = lax.dynamic_index_in_dim(total, level ^ s, 0, False)
        got = lay.levels(got, s) if s else got
        input_grad = lax.dynamic_update_slice_in_dim(input_grad, got, (level ^ s) * width, 1)
    return input_grad, new_momentum


def products(lay, sources, buffers, fills, jobs, width):
    scalars = jnp.stack([lay.place, lay.core]).astype(jnp.int32)
    block = buffers[jobs[0][0]][0]
    half = block // PLANE // 2
    piece = width // PLANE

    def kernel(scalar_ref, *refs):
        ins, refs = refs[: len(sources)], refs[len(sources):]
        keep_ref, give_ref, *scratch = refs
        buffer_refs, sems = scratch[:-1], scratch[-1]
        place, core = scalar_ref[0], scalar_ref[1]
        copies = []
        for i, (s, c0, b, r0, c1, cols) in enumerate(fills):
            n = sources[s].shape[0]
            copies.append(
                pltpu.make_async_copy(
                    ins[s].at[:, pl.ds(c0, cols)],
                    buffer_refs[b].at[pl.ds(r0, n), pl.ds(c1, cols)],
                    sems.at[i],
                )
            )
        for copy in copies:
            copy.start()
        waited = set()

        def need(ids):
            for i in ids:
                if i not in waited:
                    copies[i].wait()
                    waited.add(i)

        for at, (a, b, a0, b0, cols, a_ids, b_ids) in enumerate(jobs):
            need(a_ids)
            for r in range(PLANE):
                need(b_ids(r))
                column = at * width + pl.multiple_of((place ^ r) * piece, piece)
                for p in range(0, PLANE, 2):
                    x = nt(
                        buffer_refs[a][2 * p * half:(2 * p + 4) * half, a0:a0 + cols],
                        buffer_refs[b][r * piece:(r + 1) * piece, b0:b0 + cols],
                    ).astype(bf16)
                    for i in range(2):
                        low, high = x[2 * i * half:][:half], x[(2 * i + 1) * half:][:half]
                        keep_ref[p + i, :, pl.ds(column, piece)] = jnp.where(core == 0, low, high)
                        give_ref[p + i, :, pl.ds(column, piece)] = jnp.where(core == 0, high, low)
        need(range(len(copies)))

    out = jax.ShapeDtypeStruct((PLANE, half, len(jobs) * width), bf16)
    return pl.pallas_call(
        kernel,
        out_shape=(out, out),
        in_specs=[pl.BlockSpec(memory_space=pltpu.SMEM)]
        + [pl.BlockSpec(memory_space=pl.ANY)] * len(sources),
        out_specs=[pl.BlockSpec(memory_space=pltpu.VMEM)] * 2,
        scratch_shapes=[pltpu.VMEM(shape, bf16) for shape in buffers]
        + [pltpu.SemaphoreType.DMA((len(fills),))],
        compiler_params=pltpu.CompilerParams(vmem_limit_bytes=36 * 2**20),
        cost_estimate=pl.CostEstimate(flops=10**6, bytes_accessed=10**5, transcendentals=0),
    )(scalars, *sources)


def line_of_four(inputs, out_grad, weight, proj_basis, momentum):
    lay = Layout()
    level, across = lay.level, lay.across
    inner = (level == 1) | (level == 2)
    tokens, hidden = out_grad.shape
    rows = weight.shape[0]
    width, block, pair = rows * PLANE, tokens * PLANE, tokens * 2
    both = hidden // PLANE
    half = both // 2
    low, high = slice(0, half), slice(half, both)
    end_swap = lambda x: lay.levels(x, 1)
    mid_swap = lambda x: lay.levels(x, 3, (1, 2))
    swap = lambda x: lax.ppermute(x, "tensor", [(0, 1), (1, 0)])
    send = lambda a, w: jnp.where(inner, a, w)

    cuts = [lay.cut(out_grad, r) for r in range(PLANE)]
    plane = [across(cuts[r], r) for r in range(1, PLANE)]
    e0, m0 = end_swap(cuts[0]), mid_swap(cuts[0])
    proj = projected(lay, after(inputs, plane[0]), proj_basis)
    weight = after(weight, plane[0])
    parts = [lay.cut(weight, r) for r in range(PLANE)]
    panel = sum(tn(q, a) for q, a in zip(proj, [cuts[0], *plane]))
    panel = panel + end_swap(panel.astype(bf16)).astype(f32)
    rest = after(jnp.concatenate(plane, 0), e0, m0)
    e1, m1 = end_swap(rest), mid_swap(rest)
    parts[1:3] = [across(after(parts[r], *plane), r) for r in (1, 2)]
    parts[3] = across(after(parts[3], *parts[1:3]), 3)
    panel = (panel + lay.levels(panel.astype(bf16), 2).astype(f32)).astype(bf16)

    joined = lambda x, c: jnp.concatenate([x[0][:, c], x[1][:, c]], 0)
    near_e, near_m = [e0, e1], [m0, m1]
    e_high = joined(near_e, high)
    m_low = joined(near_m, low)
    far0 = mid_swap(joined(near_e, low))
    got_a = send(m_low, jnp.concatenate([w[:, high] for w in parts[:2]], 0))
    got_a = end_swap(got_a)
    far1, got = [], []
    for i, w in enumerate(parts[2:]):
        rows_i = slice(i * pair, (i + 1) * pair)
        far1.append(mid_swap(after(e_high[rows_i], far0, got_a)))
        got.append(end_swap(after(send(far0[rows_i], w[:, high]), got_a, parts[3], panel)))
    weight_fills = lambda first, b: [(first + r, 0, b, r * rows, 0, both) for r in range(PLANE)]
    none = lambda r: ()
    early0 = send(m_low, got_a)
    sources = [after(cuts[0], far0), rest, *near_e, early0, *near_m, *parts]
    fills = [(0, 0, 0, 0, 0, both), (1, 0, 0, tokens, 0, both)] + weight_fills(7, 3)
    fills += [(2, 0, 1, 0, 0, both), (3, 0, 1, tokens, 0, both)]
    fills += [(4, 0, 2, 0, 0, half), (5, half, 2, 0, half, half), (6, half, 2, tokens, half, half)]
    jobs = [
        (0, 3, 0, 0, both, (0, 1), lambda r: (2 + r,)),
        (1, 3, 0, 0, both, (6, 7), none),
        (2, 3, 0, 0, both, (8, 9, 10), none),
    ]
    keep, give = products(lay, sources, [(block, both)] * 3 + [(width, both)], fills, jobs, width)
    give = after(give, far1[0], got[0])
    first = (keep.astype(f32) + swap(give).astype(f32)).astype(bf16)
    first_x, first_y = across(first[1], 1), across(first[2], 2)

    late0 = send(far0, jnp.concatenate(got, 0))
    sources = [after(late0, first_x, first_y), *far1, *near_m, *parts, got_a, *got]
    fills = [(0, 0, 0, 0, 0, half)]
    fills += [(1 + i, 0, 0, i * pair, half, half) for i in range(2)]
    fills += weight_fills(5, 2)
    fills += [(3, half, 1, 0, 0, half), (4, half, 1, tokens, 0, half)]
    fills += [(9, 0, 3, 0, 0, half), (10, 0, 3, 2 * rows, 0, half), (11, 0, 3, 3 * rows, 0, half)]
    jobs = [
        (0, 2, 0, 0, both, (0, 1, 2), lambda r: (3 + r,)),
        (1, 3, 0, 0, half, (7, 8), lambda r: ((9,), (), (10,), (11,))[r]),
        (0, 3, half, 0, half, (), none),
    ]
    buffers = [(block, both), (block, half), (width, both), (width, half)]
    keep, give = products(lay, sources, buffers, fills, jobs, width)

    def plane_sum(own, *others):
        return sum(x.astype(f32) for x in (own, *others)).astype(bf16)

    first = plane_sum(first[0], first_x, first_y, after(across(first[3], 3), keep))
    second = (keep.astype(f32) + swap(give).astype(f32)).astype(bf16)
    second = plane_sum(second[0], *[across(second[r], r) for r in range(1, PLANE)])
    panel = after(panel, second)
    panel = jnp.stack([panel] + [across(panel, r) for r in range(1, PLANE)])
    panel = jnp.concatenate(
        [lax.dynamic_index_in_dim(panel, lay.place ^ p, 0, False) for p in range(PLANE)], 1
    )
    new_momentum = updated(lay, proj_basis, panel, momentum, tokens * lay.replicas)
    y0, y1, early = [first[:, i * width:(i + 1) * width] for i in range(3)]
    late, early_other, late_other = [second[:, i * width:(i + 1) * width] for i in range(3)]

    z1 = end_swap(y1)
    z3 = mid_swap(early)
    z2 = lay.levels(early, 2, (0, 3))
    late, early_other = after((late, early_other), z1, z2, z3)
    z2b = mid_swap(early_other)
    z_late = lay.levels(jnp.concatenate([late, late_other], 1), 2, (1, 2))
    z3b = lay.levels(late, 3, (0, 3))
    add = lambda *xs: sum(x.astype(f32) for x in xs).astype(bf16)
    z2 = add(z2, z2b, z_late[:, :width])
    z3 = add(z3, z3b, z_late[:, width:])
    input_grad = jnp.concatenate(
        [
            jnp.where(
                level == b,
                y0,
                jnp.where(level == b ^ 1, z1, jnp.where(level == b ^ 2, z2, z3)),
            )
            for b in range(lay.line)
        ],
        1,
    )
    return input_grad, new_momentum


def solution(mesh):
    placed = (
        P(("dp", "tensor"), None),
        P("dp", "tensor"),
        P("dp", "tensor"),
        P(),
        P("dp", "tensor"),
    )
    four = mesh.shape["dp"] == 4 * PLANE and mesh.shape["tensor"] == 2
    return jax.shard_map(
        line_of_four if four else long_line,
        mesh=mesh,
        in_specs=placed,
        out_specs=(P(("dp", "tensor"), None), P("dp", "tensor")),
        check_vma=False,
    )
```

```python
import math

import jax
import jax.numpy as jnp
from jax import lax
from jax.experimental import pallas as pl
from jax.experimental.pallas import tpu as pltpu
from jax.sharding import PartitionSpec as P

momentum_decay = 0.9
PLANE = 4
f32, bf16 = jnp.float32, jnp.bfloat16


def after(x, *first):
    return lax.optimization_barrier((x, first))[0]


def nt(a, b):
    return lax.dot_general(a, b, (((1,), (1,)), ((), ())), preferred_element_type=f32)


def tn(a, b):
    return lax.dot_general(a, b, (((0,), (0,)), ((), ())), preferred_element_type=f32)


class Layout:
    def __init__(self):
        self.replicas, self.cores = lax.axis_size("dp"), lax.axis_size("tensor")
        self.line = self.replicas // PLANE
        self.me, self.core = lax.axis_index("dp"), lax.axis_index("tensor")
        self.place, self.level = self.me % PLANE, self.me // PLANE

    def across(self, x, r):
        return lax.ppermute(x, "dp", [(d, d ^ r) for d in range(self.replicas)])

    def levels(self, x, s, only=None):
        pairs = [
            (d, d ^ (s * PLANE)) for d in range(self.replicas) if only is None or d // PLANE in only
        ]
        return lax.ppermute(x, "dp", pairs)

    def cut(self, x, r):
        quarter = x.shape[1] // PLANE
        return lax.dynamic_slice_in_dim(x, (self.place ^ r) * quarter, quarter, 1)

    def in_order(self, parts, axis):
        size = parts[0].shape[axis]
        shape = list(parts[0].shape)
        shape[axis] *= PLANE
        whole = jnp.zeros(shape, parts[0].dtype)
        for r, part in enumerate(parts):
            whole = lax.dynamic_update_slice_in_dim(whole, part, (self.place ^ r) * size, axis)
        return whole

    def core_sum(self, part, lines):
        width = part.shape[1]
        if self.cores == 2:
            part = part.reshape(lines, 2, -1, width)
            keep = lax.dynamic_index_in_dim(part, self.core, 1, False)
            give = lax.dynamic_index_in_dim(part, 1 - self.core, 1, False)
            got = lax.ppermute(give, "tensor", [(0, 1), (1, 0)])
            return (keep.astype(f32) + got.astype(f32)).astype(bf16)
        return lax.psum_scatter(
            part.reshape(lines, -1, width), "tensor", scatter_dimension=1, tiled=True
        )


def projected(lay, inputs, proj_basis):
    proj = jnp.dot(inputs.astype(f32), proj_basis, precision=lax.Precision.HIGHEST).astype(bf16)
    proj = lax.all_gather(proj, "tensor", axis=0, tiled=True)
    return [proj] + [lay.across(proj, r) for r in range(1, PLANE)]


def panel_shares(lay, plane_proj, pieces):
    panel = sum(tn(q, a) for q, a in zip(plane_proj, pieces))
    share = panel.shape[0] // lay.line
    share_of = lambda x, s: lax.dynamic_slice_in_dim(x, (lay.level ^ s) * share, share, 0)
    half = panel.astype(bf16)
    return [share_of(panel, 0)] + [lay.levels(share_of(half, s), s) for s in range(1, lay.line)]


def panel_quarter(lay, shares):
    summed = sum(x.astype(f32) for x in shares).astype(bf16)
    share, quarter = summed.shape
    panel_q = jnp.zeros((share * lay.line, quarter), bf16)
    for s in range(lay.line):
        got = lay.levels(summed, s) if s else summed
        panel_q = lax.dynamic_update_slice_in_dim(panel_q, got, (lay.level ^ s) * share, 0)
    return panel_q


def panel_whole(lay, panel_q):
    return lay.in_order([panel_q] + [lay.across(panel_q, r) for r in range(1, PLANE)], 1)


def updated(lay, proj_basis, panel, momentum, tokens):
    rows, rank = momentum.shape[0], proj_basis.shape[1]
    basis_rows = lax.dynamic_slice_in_dim(proj_basis, lay.me * rows, rows, 0)
    scale = math.sqrt(proj_basis.shape[0] / rank) / math.sqrt(tokens)
    update = jnp.dot(basis_rows.astype(bf16), panel, preferred_element_type=f32)
    return momentum_decay * momentum + update * scale


def long_line(inputs, out_grad, weight, proj_basis, momentum):
    lay = Layout()
    line, level, cores = lay.line, lay.level, lay.cores
    tokens = out_grad.shape[0]
    pieces = [lay.cut(out_grad, 0)] + [lay.across(lay.cut(out_grad, r), r) for r in range(1, PLANE)]
    weights = [lay.cut(weight, 0)] + [lay.across(lay.cut(weight, r), r) for r in range(1, PLANE)]
    groups = [[p + PLANE * z for z in range(line)] for p in range(PLANE)]
    shares = panel_shares(lay, projected(lay, inputs, proj_basis), pieces)
    panel = panel_whole(lay, panel_quarter(lay, shares))
    new_momentum = updated(lay, proj_basis, panel, momentum, tokens * lay.replicas)
    held = lay.in_order(weights, 0)
    width = held.shape[0]
    total = 0.0
    for r, piece in enumerate(pieces):
        block = lax.all_gather(piece, "dp", axis_index_groups=groups, axis=0, tiled=True)
        part = lay.core_sum(nt(block, held).astype(bf16), line)
        total = total + (lay.across(part, r) if r else part).astype(f32)
    total = total.astype(bf16)
    input_grad = jnp.zeros((tokens // cores, line * width), bf16)
    for s in range(line):
        got = lax.dynamic_index_in_dim(total, level ^ s, 0, False)
        got = lay.levels(got, s) if s else got
        input_grad = lax.dynamic_update_slice_in_dim(input_grad, got, (level ^ s) * width, 1)
    return input_grad, new_momentum


def products(lay, sources, buffers, fills, jobs, width):
    scalars = jnp.stack([lay.place, lay.core]).astype(jnp.int32)
    block = buffers[jobs[0][0]][0]
    half = block // PLANE // 2
    piece = width // PLANE

    def kernel(scalar_ref, *refs):
        ins, refs = refs[: len(sources)], refs[len(sources):]
        keep_ref, give_ref, *scratch = refs
        buffer_refs, sems = scratch[:-1], scratch[-1]
        place, core = scalar_ref[0], scalar_ref[1]
        copies = []
        for i, (s, c0, b, r0, c1, cols) in enumerate(fills):
            n = sources[s].shape[0]
            copies.append(
                pltpu.make_async_copy(
                    ins[s].at[:, pl.ds(c0, cols)],
                    buffer_refs[b].at[pl.ds(r0, n), pl.ds(c1, cols)],
                    sems.at[i],
                )
            )
        for copy in copies:
            copy.start()
        waited = set()

        def need(ids):
            for i in ids:
                if i not in waited:
                    copies[i].wait()
                    waited.add(i)

        for at, (a, b, a0, b0, cols, a_ids, b_ids) in enumerate(jobs):
            need(a_ids)
            for r in range(PLANE):
                need(b_ids(r))
                column = at * width + pl.multiple_of((place ^ r) * piece, piece)
                for p in range(0, PLANE, 2):
                    x = nt(
                        buffer_refs[a][2 * p * half:(2 * p + 4) * half, a0:a0 + cols],
                        buffer_refs[b][r * piece:(r + 1) * piece, b0:b0 + cols],
                    ).astype(bf16)
                    for i in range(2):
                        low, high = x[2 * i * half:][:half], x[(2 * i + 1) * half:][:half]
                        keep_ref[p + i, :, pl.ds(column, piece)] = jnp.where(core == 0, low, high)
                        give_ref[p + i, :, pl.ds(column, piece)] = jnp.where(core == 0, high, low)
        need(range(len(copies)))

    out = jax.ShapeDtypeStruct((PLANE, half, len(jobs) * width), bf16)
    return pl.pallas_call(
        kernel,
        out_shape=(out, out),
        in_specs=[pl.BlockSpec(memory_space=pltpu.SMEM)]
        + [pl.BlockSpec(memory_space=pl.ANY)] * len(sources),
        out_specs=[pl.BlockSpec(memory_space=pltpu.VMEM)] * 2,
        scratch_shapes=[pltpu.VMEM(shape, bf16) for shape in buffers]
        + [pltpu.SemaphoreType.DMA((len(fills),))],
        compiler_params=pltpu.CompilerParams(vmem_limit_bytes=36 * 2**20),
        cost_estimate=pl.CostEstimate(flops=10**6, bytes_accessed=10**5, transcendentals=0),
    )(scalars, *sources)


def line_of_four(inputs, out_grad, weight, proj_basis, momentum):
    lay = Layout()
    level, across = lay.level, lay.across
    inner = (level == 1) | (level == 2)
    tokens, hidden = out_grad.shape
    rows = weight.shape[0]
    width, block = rows * PLANE, tokens * PLANE
    both = hidden // PLANE
    half = both // 2
    low, high = slice(0, half), slice(half, both)
    end_swap = lambda x: lay.levels(x, 1)
    mid_swap = lambda x: lay.levels(x, 3, (1, 2))
    swap = lambda x: lax.ppermute(x, "tensor", [(0, 1), (1, 0)])
    send = lambda a, w: jnp.where(inner, a, w)

    cuts = [lay.cut(out_grad, r) for r in range(PLANE)]
    plane = [across(cuts[r], r) for r in (1, 2)]
    e0, m0 = end_swap(cuts[0]), mid_swap(cuts[0])
    plane.append(across(after(cuts[3], *plane), 3))
    weight = after(weight, e0, m0)
    parts = [lay.cut(weight, r) for r in range(PLANE)]
    sides = after(jnp.concatenate(plane[:2], 0), e0, m0)
    e1, m1 = end_swap(sides), mid_swap(sides)
    e2, m2 = end_swap(plane[2]), mid_swap(plane[2])
    parts[1:3] = [across(after(parts[r], *plane), r) for r in (1, 2)]
    parts[3] = across(after(parts[3], *parts[1:3]), 3)
    joined = lambda x, c: jnp.concatenate([y[:, c] for y in x], 0)
    near_e, near_m = [e0, e1, e2], [m0, m1, m2]
    e_high = joined(near_e, high)
    m_low = joined(near_m, low)
    far0 = mid_swap(joined(near_e, low))
    got_a = send(m_low, jnp.concatenate([w[:, high] for w in parts[:2]], 0))
    got_a = end_swap(got_a)
    proj = projected(lay, after(inputs, e1, m1), proj_basis)
    far1, got = [], []
    for i, w in enumerate(parts[2:]):
        rows_i = slice(i * 2 * tokens, (i + 1) * 2 * tokens)
        far1.append(mid_swap(after(e_high[rows_i], far0, got_a)))
        got.append(end_swap(after(send(far0[rows_i], w[:, high]), got_a, parts[3], *proj)))

    weight_fills = lambda first, b: [(first + r, 0, b, r * rows, 0, both) for r in range(PLANE)]
    none = lambda r: ()
    early0 = send(m_low, got_a)
    own = [after(cuts[0], far0), sides, plane[2]]
    sources = [*own, *near_e, early0, *near_m, *parts]
    starts = (0, tokens, 3 * tokens)
    fills = [(i, 0, 0, row, 0, both) for i, row in enumerate(starts)] + weight_fills(10, 3)
    fills += [(3 + i, 0, 1, row, 0, both) for i, row in enumerate(starts)]
    fills += [(6, 0, 2, 0, 0, half)]
    fills += [(7 + i, half, 2, row, half, half) for i, row in enumerate(starts)]
    jobs = [
        (0, 3, 0, 0, both, (0, 1, 2), lambda r: (3 + r,)),
        (1, 3, 0, 0, both, (7, 8, 9), none),
        (2, 3, 0, 0, both, (10, 11, 12, 13), none),
    ]
    keep, give = products(lay, sources, [(block, both)] * 3 + [(width, both)], fills, jobs, width)
    give = after(give, far1[0], got[0])
    first = (keep.astype(f32) + swap(give).astype(f32)).astype(bf16)
    first_x, first_y = across(first[1], 1), across(first[2], 2)

    panel = sum(tn(q, a) for q, a in zip(proj, [after(cuts[0], give), *plane]))
    panel = panel + end_swap(after(panel.astype(bf16), first)).astype(f32)

    late0 = send(far0, jnp.concatenate(got, 0))
    sources = [after(late0, first), *far1, *near_m, *parts, got_a, *got]
    fills = [(0, 0, 0, 0, 0, half)]
    fills += [(1 + i, 0, 0, 2 * i * tokens, half, half) for i in range(2)] + weight_fills(6, 2)
    fills += [(3 + i, half, 1, row, 0, half) for i, row in enumerate(starts)]
    fills += [(10, 0, 3, 0, 0, half), (11, 0, 3, 2 * rows, 0, half), (12, 0, 3, 3 * rows, 0, half)]
    jobs = [
        (0, 2, 0, 0, both, (0, 1, 2), lambda r: (3 + r,)),
        (1, 3, 0, 0, half, (7, 8, 9), lambda r: ((10,), (), (11,), (12,))[r]),
        (0, 3, half, 0, half, (), none),
    ]
    buffers = [(block, both), (block, half), (width, both), (width, half)]
    keep, give = products(lay, sources, buffers, fills, jobs, width)

    def plane_sum(own, *others):
        return sum(x.astype(f32) for x in (own, *others)).astype(bf16)

    first = plane_sum(first[0], first_x, first_y, across(first[3], 3))
    give = after(give, first)
    second = (keep.astype(f32) + swap(give).astype(f32)).astype(bf16)
    second = plane_sum(second[0], *[across(second[r], r) for r in range(1, PLANE)])
    panel = (panel + lay.levels(after(panel.astype(bf16), second), 2).astype(f32)).astype(bf16)
    summed_panel = panel
    panel = jnp.stack([panel] + [across(panel, r) for r in range(1, PLANE)])
    panel = jnp.concatenate(
        [lax.dynamic_index_in_dim(panel, lay.place ^ p, 0, False) for p in range(PLANE)], 1
    )
    new_momentum = updated(lay, proj_basis, panel, momentum, tokens * lay.replicas)
    y0, y1, early = [first[:, i * width:(i + 1) * width] for i in range(3)]
    late, early_other, late_other = [second[:, i * width:(i + 1) * width] for i in range(3)]

    z1 = end_swap(y1)
    z3 = mid_swap(early)
    z2 = lay.levels(early, 2, (0, 3))
    late, early_other = after((late, early_other), z1, z2, z3, summed_panel)
    z2b = mid_swap(early_other)
    z_late = lay.levels(jnp.concatenate([late, late_other], 1), 2, (1, 2))
    z3b = lay.levels(late, 3, (0, 3))
    add = lambda *xs: sum(x.astype(f32) for x in xs).astype(bf16)
    z2 = add(z2, z2b, z_late[:, :width])
    z3 = add(z3, z3b, z_late[:, width:])
    input_grad = jnp.concatenate(
        [
            jnp.where(
                level == b,
                y0,
                jnp.where(level == b ^ 1, z1, jnp.where(level == b ^ 2, z2, z3)),
            )
            for b in range(lay.line)
        ],
        1,
    )
    return input_grad, new_momentum


def solution(mesh):
    placed = (
        P(("dp", "tensor"), None),
        P("dp", "tensor"),
        P("dp", "tensor"),
        P(),
        P("dp", "tensor"),
    )
    four = mesh.shape["dp"] == 4 * PLANE and mesh.shape["tensor"] == 2
    return jax.shard_map(
        line_of_four if four else long_line,
        mesh=mesh,
        in_specs=placed,
        out_specs=(P(("dp", "tensor"), None), P("dp", "tensor")),
        check_vma=False,
    )
```

```python
import math

import jax
import jax.numpy as jnp
from jax import lax
from jax.experimental import pallas as pl
from jax.experimental.pallas import tpu as pltpu
from jax.sharding import PartitionSpec as P

momentum_decay = 0.9
PLANE = 4
f32, bf16 = jnp.float32, jnp.bfloat16


def after(x, *first):
    return lax.optimization_barrier((x, first))[0]


def nt(a, b):
    return lax.dot_general(a, b, (((1,), (1,)), ((), ())), preferred_element_type=f32)


def tn(a, b):
    return lax.dot_general(a, b, (((0,), (0,)), ((), ())), preferred_element_type=f32)


class Layout:
    def __init__(self):
        self.replicas, self.cores = lax.axis_size("dp"), lax.axis_size("tensor")
        self.line = self.replicas // PLANE
        self.me, self.core = lax.axis_index("dp"), lax.axis_index("tensor")
        self.place, self.level = self.me % PLANE, self.me // PLANE

    def across(self, x, r):
        return lax.ppermute(x, "dp", [(d, d ^ r) for d in range(self.replicas)])

    def levels(self, x, s, only=None):
        pairs = [
            (d, d ^ (s * PLANE)) for d in range(self.replicas) if only is None or d // PLANE in only
        ]
        return lax.ppermute(x, "dp", pairs)

    def cut(self, x, r):
        quarter = x.shape[1] // PLANE
        return lax.dynamic_slice_in_dim(x, (self.place ^ r) * quarter, quarter, 1)

    def in_order(self, parts, axis):
        size = parts[0].shape[axis]
        shape = list(parts[0].shape)
        shape[axis] *= PLANE
        whole = jnp.zeros(shape, parts[0].dtype)
        for r, part in enumerate(parts):
            whole = lax.dynamic_update_slice_in_dim(whole, part, (self.place ^ r) * size, axis)
        return whole

    def core_sum(self, part, lines):
        width = part.shape[1]
        if self.cores == 2:
            part = part.reshape(lines, 2, -1, width)
            keep = lax.dynamic_index_in_dim(part, self.core, 1, False)
            give = lax.dynamic_index_in_dim(part, 1 - self.core, 1, False)
            got = lax.ppermute(give, "tensor", [(0, 1), (1, 0)])
            return (keep.astype(f32) + got.astype(f32)).astype(bf16)
        return lax.psum_scatter(
            part.reshape(lines, -1, width), "tensor", scatter_dimension=1, tiled=True
        )


def projected(lay, inputs, proj_basis):
    proj = jnp.dot(inputs.astype(f32), proj_basis, precision=lax.Precision.HIGHEST).astype(bf16)
    proj = lax.all_gather(proj, "tensor", axis=0, tiled=True)
    return [proj] + [lay.across(proj, r) for r in range(1, PLANE)]


def panel_shares(lay, plane_proj, pieces):
    panel = sum(tn(q, a) for q, a in zip(plane_proj, pieces))
    share = panel.shape[0] // lay.line
    share_of = lambda x, s: lax.dynamic_slice_in_dim(x, (lay.level ^ s) * share, share, 0)
    half = panel.astype(bf16)
    return [share_of(panel, 0)] + [lay.levels(share_of(half, s), s) for s in range(1, lay.line)]


def panel_quarter(lay, shares):
    summed = sum(x.astype(f32) for x in shares).astype(bf16)
    share, quarter = summed.shape
    panel_q = jnp.zeros((share * lay.line, quarter), bf16)
    for s in range(lay.line):
        got = lay.levels(summed, s) if s else summed
        panel_q = lax.dynamic_update_slice_in_dim(panel_q, got, (lay.level ^ s) * share, 0)
    return panel_q


def panel_whole(lay, panel_q):
    return lay.in_order([panel_q] + [lay.across(panel_q, r) for r in range(1, PLANE)], 1)


def updated(lay, proj_basis, panel, momentum, tokens):
    rows, rank = momentum.shape[0], proj_basis.shape[1]
    basis_rows = lax.dynamic_slice_in_dim(proj_basis, lay.me * rows, rows, 0)
    scale = math.sqrt(proj_basis.shape[0] / rank) / math.sqrt(tokens)
    update = jnp.dot(basis_rows.astype(bf16), panel, preferred_element_type=f32)
    return momentum_decay * momentum + update * scale


def long_line(inputs, out_grad, weight, proj_basis, momentum):
    lay = Layout()
    line, level, cores = lay.line, lay.level, lay.cores
    tokens = out_grad.shape[0]
    pieces = [lay.cut(out_grad, 0)] + [lay.across(lay.cut(out_grad, r), r) for r in range(1, PLANE)]
    weights = [lay.cut(weight, 0)] + [lay.across(lay.cut(weight, r), r) for r in range(1, PLANE)]
    groups = [[p + PLANE * z for z in range(line)] for p in range(PLANE)]
    shares = panel_shares(lay, projected(lay, inputs, proj_basis), pieces)
    panel = panel_whole(lay, panel_quarter(lay, shares))
    new_momentum = updated(lay, proj_basis, panel, momentum, tokens * lay.replicas)
    held = lay.in_order(weights, 0)
    width = held.shape[0]
    total = 0.0
    for r, piece in enumerate(pieces):
        block = lax.all_gather(piece, "dp", axis_index_groups=groups, axis=0, tiled=True)
        part = lay.core_sum(nt(block, held).astype(bf16), line)
        total = total + (lay.across(part, r) if r else part).astype(f32)
    total = total.astype(bf16)
    input_grad = jnp.zeros((tokens // cores, line * width), bf16)
    for s in range(line):
        got = lax.dynamic_index_in_dim(total, level ^ s, 0, False)
        got = lay.levels(got, s) if s else got
        input_grad = lax.dynamic_update_slice_in_dim(input_grad, got, (level ^ s) * width, 1)
    return input_grad, new_momentum


def products(lay, sources, buffers, fills, jobs, width):
    scalars = jnp.stack([lay.place, lay.core]).astype(jnp.int32)
    block = buffers[jobs[0][0]][0]
    half = block // PLANE // 2
    piece = width // PLANE

    def kernel(scalar_ref, *refs):
        ins, refs = refs[: len(sources)], refs[len(sources):]
        keep_ref, give_ref, *scratch = refs
        buffer_refs, sems = scratch[:-1], scratch[-1]
        place, core = scalar_ref[0], scalar_ref[1]
        copies = []
        for i, (s, c0, b, r0, c1, cols) in enumerate(fills):
            n = sources[s].shape[0]
            copies.append(
                pltpu.make_async_copy(
                    ins[s].at[:, pl.ds(c0, cols)],
                    buffer_refs[b].at[pl.ds(r0, n), pl.ds(c1, cols)],
                    sems.at[i],
                )
            )
        for copy in copies:
            copy.start()
        waited = set()

        def need(ids):
            for i in ids:
                if i not in waited:
                    copies[i].wait()
                    waited.add(i)

        for at, (a, b, a0, b0, cols, a_ids, b_ids) in enumerate(jobs):
            need(a_ids)
            for r in range(PLANE):
                need(b_ids(r))
                column = at * width + pl.multiple_of((place ^ r) * piece, piece)
                for p in range(PLANE):
                    x = nt(
                        buffer_refs[a][2 * p * half:(2 * p + 2) * half, a0:a0 + cols],
                        buffer_refs[b][r * piece:(r + 1) * piece, b0:b0 + cols],
                    ).astype(bf16)
                    low, high = x[:half], x[half:]
                    keep_ref[p, :, pl.ds(column, piece)] = jnp.where(core == 0, low, high)
                    give_ref[p, :, pl.ds(column, piece)] = jnp.where(core == 0, high, low)
        need(range(len(copies)))

    out = jax.ShapeDtypeStruct((PLANE, half, len(jobs) * width), bf16)
    return pl.pallas_call(
        kernel,
        out_shape=(out, out),
        in_specs=[pl.BlockSpec(memory_space=pltpu.SMEM)]
        + [pl.BlockSpec(memory_space=pl.ANY)] * len(sources),
        out_specs=[pl.BlockSpec(memory_space=pltpu.VMEM)] * 2,
        scratch_shapes=[pltpu.VMEM(shape, bf16) for shape in buffers]
        + [pltpu.SemaphoreType.DMA((len(fills),))],
        compiler_params=pltpu.CompilerParams(vmem_limit_bytes=36 * 2**20),
        cost_estimate=pl.CostEstimate(flops=10**6, bytes_accessed=10**5, transcendentals=0),
    )(scalars, *sources)


def line_of_four(inputs, out_grad, weight, proj_basis, momentum):
    lay = Layout()
    level, across = lay.level, lay.across
    inner = (level == 1) | (level == 2)
    tokens, hidden = out_grad.shape
    rows = weight.shape[0]
    width, block = rows * PLANE, tokens * PLANE
    both = hidden // PLANE
    half = both // 2
    low, high = slice(0, half), slice(half, both)
    end_swap = lambda x: lay.levels(x, 1)
    mid_swap = lambda x: lay.levels(x, 3, (1, 2))
    swap = lambda x: lax.ppermute(x, "tensor", [(0, 1), (1, 0)])
    send = lambda a, w: jnp.where(inner, a, w)

    cuts = [lay.cut(out_grad, r) for r in range(PLANE)]
    plane = [across(cuts[r], r) for r in (1, 2)]
    e0, m0 = end_swap(cuts[0]), mid_swap(cuts[0])
    plane.append(across(after(cuts[3], *plane), 3))
    weight = after(weight, e0, m0)
    parts = [lay.cut(weight, r) for r in range(PLANE)]
    sides = after(jnp.concatenate(plane[:2], 0), e0, m0)
    e1, e2 = end_swap(sides), end_swap(plane[2])
    m1 = mid_swap(jnp.concatenate([sides, plane[2]], 0))
    parts[1:3] = [across(after(parts[r], *plane), r) for r in (1, 2)]
    parts[3] = across(after(parts[3], *parts[1:3]), 3)
    joined = lambda x, c: jnp.concatenate([y[:, c] for y in x], 0)
    near_e, near_m = [e0, e1, e2], [m0, m1]
    e_high = joined(near_e, high)
    m_low = joined(near_m, low)
    far0 = mid_swap(joined(near_e, low))
    got_a = send(m_low, jnp.concatenate([w[:, high] for w in parts[:2]], 0))
    got_a = end_swap(got_a)
    proj = projected(lay, after(inputs, e1, m1), proj_basis)
    far1, got = [], []
    for i, w in enumerate(parts[2:]):
        rows_i = slice(i * 2 * tokens, (i + 1) * 2 * tokens)
        far1.append(mid_swap(after(e_high[rows_i], far0, got_a)))
        got.append(end_swap(after(send(far0[rows_i], w[:, high]), got_a, parts[3], *proj)))

    weight_fills = lambda first, b: [(first + r, 0, b, r * rows, 0, both) for r in range(PLANE)]
    none = lambda r: ()
    early0 = send(m_low, got_a)
    own = [after(cuts[0], far0), sides, plane[2]]
    sources = [*own, *near_e, early0, *near_m, *parts]
    starts = (0, tokens, 3 * tokens)
    fills = [(i, 0, 0, row, 0, both) for i, row in enumerate(starts)] + weight_fills(9, 3)
    fills += [(3 + i, 0, 1, row, 0, both) for i, row in enumerate(starts)]
    fills += [(6, 0, 2, 0, 0, half)]
    fills += [(7, half, 2, 0, half, half), (8, half, 2, tokens, half, half)]
    jobs = [
        (0, 3, 0, 0, both, (0, 1, 2), lambda r: (3 + r,)),
        (1, 3, 0, 0, both, (7, 8, 9), none),
        (2, 3, 0, 0, both, (10, 11, 12), none),
    ]
    keep, give = products(lay, sources, [(block, both)] * 3 + [(width, both)], fills, jobs, width)
    give = after(give, far1[0], got[0])
    first = (keep.astype(f32) + swap(give).astype(f32)).astype(bf16)
    first_x, first_y = across(first[1], 1), across(first[2], 2)

    panel = sum(tn(q, a) for q, a in zip(proj, [after(cuts[0], give), *plane]))
    panel = panel + end_swap(after(panel.astype(bf16), first)).astype(f32)

    late0 = send(far0, jnp.concatenate(got, 0))
    sources = [late0, *far1, after(m0, first, panel), m1, *parts, got_a, *got]
    fills = [(0, 0, 0, 0, 0, half)]
    fills += [(1 + i, 0, 0, 2 * i * tokens, half, half) for i in range(2)] + weight_fills(5, 2)
    fills += [(3, half, 1, 0, 0, half), (4, half, 1, tokens, 0, half)]
    fills += [(9, 0, 3, 0, 0, half), (10, 0, 3, 2 * rows, 0, half), (11, 0, 3, 3 * rows, 0, half)]
    jobs = [
        (0, 2, 0, 0, both, (0, 1, 2), lambda r: (3 + r,)),
        (1, 3, 0, 0, half, (7, 8), lambda r: ((9,), (), (10,), (11,))[r]),
        (0, 3, half, 0, half, (), none),
    ]
    buffers = [(block, both), (block, half), (width, both), (width, half)]
    keep, give = products(lay, sources, buffers, fills, jobs, width)

    def plane_sum(own, *others):
        return sum(x.astype(f32) for x in (own, *others)).astype(bf16)

    first = plane_sum(first[0], first_x, first_y, across(first[3], 3))
    panel = (panel + lay.levels(panel.astype(bf16), 2).astype(f32)).astype(bf16)
    give = after(give, first, panel)
    second = (keep.astype(f32) + swap(give).astype(f32)).astype(bf16)
    second = plane_sum(second[0], *[across(second[r], r) for r in range(1, PLANE)])
    panel = after(panel, second)
    panel = jnp.stack([panel] + [across(panel, r) for r in range(1, PLANE)])
    panel = jnp.concatenate(
        [lax.dynamic_index_in_dim(panel, lay.place ^ p, 0, False) for p in range(PLANE)], 1
    )
    new_momentum = updated(lay, proj_basis, panel, momentum, tokens * lay.replicas)
    y0, y1, early = [first[:, i * width:(i + 1) * width] for i in range(3)]
    late, early_other, late_other = [second[:, i * width:(i + 1) * width] for i in range(3)]

    z1 = end_swap(y1)
    z3 = mid_swap(early)
    z2 = lay.levels(early, 2, (0, 3))
    late, early_other = after((late, early_other), z1, z2, z3)
    z2b = mid_swap(early_other)
    z_late = lay.levels(jnp.concatenate([late, late_other], 1), 2, (1, 2))
    z3b = lay.levels(late, 3, (0, 3))
    add = lambda *xs: sum(x.astype(f32) for x in xs).astype(bf16)
    z2 = add(z2, z2b, z_late[:, :width])
    z3 = add(z3, z3b, z_late[:, width:])
    input_grad = jnp.concatenate(
        [
            jnp.where(
                level == b,
                y0,
                jnp.where(level == b ^ 1, z1, jnp.where(level == b ^ 2, z2, z3)),
            )
            for b in range(lay.line)
        ],
        1,
    )
    return input_grad, new_momentum


def solution(mesh):
    placed = (
        P(("dp", "tensor"), None),
        P("dp", "tensor"),
        P("dp", "tensor"),
        P(),
        P("dp", "tensor"),
    )
    four = mesh.shape["dp"] == 4 * PLANE and mesh.shape["tensor"] == 2
    return jax.shard_map(
        line_of_four if four else long_line,
        mesh=mesh,
        in_specs=placed,
        out_specs=(P(("dp", "tensor"), None), P("dp", "tensor")),
        check_vma=False,
    )
```

```python
import math

import jax
import jax.numpy as jnp
from jax import lax
from jax.experimental import pallas as pl
from jax.experimental.pallas import tpu as pltpu
from jax.sharding import PartitionSpec as P

momentum_decay = 0.9
PLANE = 4
f32, bf16 = jnp.float32, jnp.bfloat16


def after(x, *first):
    return lax.optimization_barrier((x, first))[0]


def nt(a, b):
    return lax.dot_general(a, b, (((1,), (1,)), ((), ())), preferred_element_type=f32)


def tn(a, b):
    return lax.dot_general(a, b, (((0,), (0,)), ((), ())), preferred_element_type=f32)


class Layout:
    def __init__(self):
        self.replicas, self.cores = lax.axis_size("dp"), lax.axis_size("tensor")
        self.line = self.replicas // PLANE
        self.me, self.core = lax.axis_index("dp"), lax.axis_index("tensor")
        self.place, self.level = self.me % PLANE, self.me // PLANE

    def across(self, x, r):
        return lax.ppermute(x, "dp", [(d, d ^ r) for d in range(self.replicas)])

    def levels(self, x, s, only=None):
        pairs = [
            (d, d ^ (s * PLANE)) for d in range(self.replicas) if only is None or d // PLANE in only
        ]
        return lax.ppermute(x, "dp", pairs)

    def cut(self, x, r):
        quarter = x.shape[1] // PLANE
        return lax.dynamic_slice_in_dim(x, (self.place ^ r) * quarter, quarter, 1)

    def in_order(self, parts, axis):
        size = parts[0].shape[axis]
        shape = list(parts[0].shape)
        shape[axis] *= PLANE
        whole = jnp.zeros(shape, parts[0].dtype)
        for r, part in enumerate(parts):
            whole = lax.dynamic_update_slice_in_dim(whole, part, (self.place ^ r) * size, axis)
        return whole

    def core_sum(self, part, lines):
        width = part.shape[1]
        if self.cores == 2:
            part = part.reshape(lines, 2, -1, width)
            keep = lax.dynamic_index_in_dim(part, self.core, 1, False)
            give = lax.dynamic_index_in_dim(part, 1 - self.core, 1, False)
            got = lax.ppermute(give, "tensor", [(0, 1), (1, 0)])
            return (keep.astype(f32) + got.astype(f32)).astype(bf16)
        return lax.psum_scatter(
            part.reshape(lines, -1, width), "tensor", scatter_dimension=1, tiled=True
        )


def projected(lay, inputs, proj_basis):
    proj = jnp.dot(inputs.astype(f32), proj_basis, precision=lax.Precision.HIGHEST).astype(bf16)
    proj = lax.all_gather(proj, "tensor", axis=0, tiled=True)
    return [proj] + [lay.across(proj, r) for r in range(1, PLANE)]


def panel_shares(lay, plane_proj, pieces):
    panel = sum(tn(q, a) for q, a in zip(plane_proj, pieces))
    share = panel.shape[0] // lay.line
    share_of = lambda x, s: lax.dynamic_slice_in_dim(x, (lay.level ^ s) * share, share, 0)
    half = panel.astype(bf16)
    return [share_of(panel, 0)] + [lay.levels(share_of(half, s), s) for s in range(1, lay.line)]


def panel_quarter(lay, shares):
    summed = sum(x.astype(f32) for x in shares).astype(bf16)
    share, quarter = summed.shape
    panel_q = jnp.zeros((share * lay.line, quarter), bf16)
    for s in range(lay.line):
        got = lay.levels(summed, s) if s else summed
        panel_q = lax.dynamic_update_slice_in_dim(panel_q, got, (lay.level ^ s) * share, 0)
    return panel_q


def panel_whole(lay, panel_q):
    return lay.in_order([panel_q] + [lay.across(panel_q, r) for r in range(1, PLANE)], 1)


def updated(lay, proj_basis, panel, momentum, tokens):
    rows, rank = momentum.shape[0], proj_basis.shape[1]
    basis_rows = lax.dynamic_slice_in_dim(proj_basis, lay.me * rows, rows, 0)
    scale = math.sqrt(proj_basis.shape[0] / rank) / math.sqrt(tokens)
    update = jnp.dot(basis_rows.astype(bf16), panel, preferred_element_type=f32)
    return momentum_decay * momentum + update * scale


def long_line(inputs, out_grad, weight, proj_basis, momentum):
    lay = Layout()
    line, level, cores = lay.line, lay.level, lay.cores
    tokens = out_grad.shape[0]
    pieces = [lay.cut(out_grad, 0)] + [lay.across(lay.cut(out_grad, r), r) for r in range(1, PLANE)]
    weights = [lay.cut(weight, 0)] + [lay.across(lay.cut(weight, r), r) for r in range(1, PLANE)]
    groups = [[p + PLANE * z for z in range(line)] for p in range(PLANE)]
    shares = panel_shares(lay, projected(lay, inputs, proj_basis), pieces)
    panel = panel_whole(lay, panel_quarter(lay, shares))
    new_momentum = updated(lay, proj_basis, panel, momentum, tokens * lay.replicas)
    held = lay.in_order(weights, 0)
    width = held.shape[0]
    total = 0.0
    for r, piece in enumerate(pieces):
        block = lax.all_gather(piece, "dp", axis_index_groups=groups, axis=0, tiled=True)
        part = lay.core_sum(nt(block, held).astype(bf16), line)
        total = total + (lay.across(part, r) if r else part).astype(f32)
    total = total.astype(bf16)
    input_grad = jnp.zeros((tokens // cores, line * width), bf16)
    for s in range(line):
        got = lax.dynamic_index_in_dim(total, level ^ s, 0, False)
        got = lay.levels(got, s) if s else got
        input_grad = lax.dynamic_update_slice_in_dim(input_grad, got, (level ^ s) * width, 1)
    return input_grad, new_momentum


def products(lay, sources, buffers, fills, jobs, width):
    scalars = jnp.stack([lay.place, lay.core]).astype(jnp.int32)
    block = buffers[jobs[0][0]][0]
    half = block // PLANE // 2
    piece = width // PLANE

    def kernel(scalar_ref, *refs):
        ins, refs = refs[: len(sources)], refs[len(sources):]
        keep_ref, give_ref, *scratch = refs
        buffer_refs, sems = scratch[:-1], scratch[-1]
        place, core = scalar_ref[0], scalar_ref[1]
        copies = []
        for i, (s, c0, b, r0, c1, cols) in enumerate(fills):
            n = sources[s].shape[0]
            copies.append(
                pltpu.make_async_copy(
                    ins[s].at[:, pl.ds(c0, cols)],
                    buffer_refs[b].at[pl.ds(r0, n), pl.ds(c1, cols)],
                    sems.at[i],
                )
            )
        for copy in copies:
            copy.start()
        waited = set()

        def need(ids):
            for i in ids:
                if i not in waited:
                    copies[i].wait()
                    waited.add(i)

        for at, (a, b, a0, b0, cols, a_ids, b_ids) in enumerate(jobs):
            need(a_ids)
            for r in range(PLANE):
                need(b_ids(r))
                column = at * width + pl.multiple_of((place ^ r) * piece, piece)
                for p in range(0, PLANE, 2):
                    x = nt(
                        buffer_refs[a][2 * p * half:(2 * p + 4) * half, a0:a0 + cols],
                        buffer_refs[b][r * piece:(r + 1) * piece, b0:b0 + cols],
                    ).astype(bf16)
                    for i in range(2):
                        low, high = x[2 * i * half:][:half], x[(2 * i + 1) * half:][:half]
                        keep_ref[p + i, :, pl.ds(column, piece)] = jnp.where(core == 0, low, high)
                        give_ref[p + i, :, pl.ds(column, piece)] = jnp.where(core == 0, high, low)
        need(range(len(copies)))

    out = jax.ShapeDtypeStruct((PLANE, half, len(jobs) * width), bf16)
    return pl.pallas_call(
        kernel,
        out_shape=(out, out),
        in_specs=[pl.BlockSpec(memory_space=pltpu.SMEM)]
        + [pl.BlockSpec(memory_space=pl.ANY)] * len(sources),
        out_specs=[pl.BlockSpec(memory_space=pltpu.VMEM)] * 2,
        scratch_shapes=[pltpu.VMEM(shape, bf16) for shape in buffers]
        + [pltpu.SemaphoreType.DMA((len(fills),))],
        compiler_params=pltpu.CompilerParams(vmem_limit_bytes=36 * 2**20),
        cost_estimate=pl.CostEstimate(flops=10**6, bytes_accessed=10**5, transcendentals=0),
    )(scalars, *sources)


def line_of_four(inputs, out_grad, weight, proj_basis, momentum):
    lay = Layout()
    level, across = lay.level, lay.across
    inner = (level == 1) | (level == 2)
    tokens, hidden = out_grad.shape
    rows = weight.shape[0]
    width, block = rows * PLANE, tokens * PLANE
    both = hidden // PLANE
    half = both // 2
    low, high = slice(0, half), slice(half, both)
    end_swap = lambda x: lay.levels(x, 1)
    mid_swap = lambda x: lay.levels(x, 3, (1, 2))
    swap = lambda x: lax.ppermute(x, "tensor", [(0, 1), (1, 0)])
    send = lambda a, w: jnp.where(inner, a, w)

    cuts = [lay.cut(out_grad, r) for r in range(PLANE)]
    plane = [across(cuts[r], r) for r in (1, 2)]
    e0, m0 = end_swap(cuts[0]), mid_swap(cuts[0])
    plane.append(across(after(cuts[3], *plane), 3))
    weight = after(weight, e0, m0)
    parts = [lay.cut(weight, r) for r in range(PLANE)]
    sides = after(jnp.concatenate(plane[:2], 0), e0, m0)
    e1, m1 = end_swap(sides), mid_swap(sides)
    m2 = mid_swap(plane[2])
    e2 = after(end_swap(plane[2]), m2)
    parts[1:3] = [across(after(parts[r], *plane), r) for r in (1, 2)]
    parts[3] = across(after(parts[3], *parts[1:3]), 3)
    joined = lambda x, c: jnp.concatenate([y[:, c] for y in x], 0)
    near_e, near_m = [e0, e1, e2], [m0, m1, m2]
    e_high = joined(near_e, high)
    m_low = joined(near_m, low)
    far0 = mid_swap(joined(near_e, low))
    got_a = send(m_low, jnp.concatenate([w[:, high] for w in parts[:2]], 0))
    got_a = end_swap(got_a)
    proj = projected(lay, after(inputs, e1, m1), proj_basis)
    far1, got = [], []
    for i, w in enumerate(parts[2:]):
        rows_i = slice(i * 2 * tokens, (i + 1) * 2 * tokens)
        far1.append(mid_swap(after(e_high[rows_i], far0, got_a)))
        got.append(end_swap(after(send(far0[rows_i], w[:, high]), got_a, parts[3], *proj)))

    weight_fills = lambda first, b: [(first + r, 0, b, r * rows, 0, both) for r in range(PLANE)]
    none = lambda r: ()
    early0 = send(m_low, got_a)
    own = [after(cuts[0], far0), sides, plane[2]]
    sources = [*own, *near_e, early0, *near_m, *parts]
    starts = (0, tokens, 3 * tokens)
    fills = [(i, 0, 0, row, 0, both) for i, row in enumerate(starts)] + weight_fills(10, 3)
    fills += [(3 + i, 0, 1, row, 0, both) for i, row in enumerate(starts)]
    fills += [(6, 0, 2, 0, 0, half)]
    fills += [(7 + i, half, 2, row, half, half) for i, row in enumerate(starts)]
    jobs = [
        (0, 3, 0, 0, both, (0, 1, 2), lambda r: (3 + r,)),
        (1, 3, 0, 0, both, (7, 8, 9), none),
        (2, 3, 0, 0, both, (10, 11, 12, 13), none),
    ]
    keep, give = products(lay, sources, [(block, both)] * 3 + [(width, both)], fills, jobs, width)
    give = after(give, far1[0], got[0])
    first = (keep.astype(f32) + swap(give).astype(f32)).astype(bf16)
    first_x, first_y = across(first[1], 1), across(first[2], 2)

    panel = sum(tn(q, a) for q, a in zip(proj, [after(cuts[0], give), *plane]))
    panel = panel + end_swap(after(panel.astype(bf16), first)).astype(f32)

    late0 = send(far0, jnp.concatenate(got, 0))
    sources = [after(late0, first), *far1, *near_m, *parts, got_a, *got]
    fills = [(0, 0, 0, 0, 0, half)]
    fills += [(1 + i, 0, 0, 2 * i * tokens, half, half) for i in range(2)] + weight_fills(6, 2)
    fills += [(3 + i, half, 1, row, 0, half) for i, row in enumerate(starts)]
    fills += [(10, 0, 3, 0, 0, half), (11, 0, 3, 2 * rows, 0, half), (12, 0, 3, 3 * rows, 0, half)]
    jobs = [
        (0, 2, 0, 0, both, (0, 1, 2), lambda r: (3 + r,)),
        (1, 3, 0, 0, half, (7, 8, 9), lambda r: ((10,), (), (11,), (12,))[r]),
        (0, 3, half, 0, half, (), none),
    ]
    buffers = [(block, both), (block, half), (width, both), (width, half)]
    keep, give = products(lay, sources, buffers, fills, jobs, width)

    def plane_sum(own, *others):
        return sum(x.astype(f32) for x in (own, *others)).astype(bf16)

    first = plane_sum(first[0], first_x, first_y, across(first[3], 3))
    give = after(give, first)
    second = (keep.astype(f32) + swap(give).astype(f32)).astype(bf16)
    second = plane_sum(second[0], *[across(second[r], r) for r in range(1, PLANE)])
    panel = (panel + lay.levels(after(panel.astype(bf16), second), 2).astype(f32)).astype(bf16)
    panel = jnp.stack([panel] + [across(panel, r) for r in range(1, PLANE)])
    panel = jnp.concatenate(
        [lax.dynamic_index_in_dim(panel, lay.place ^ p, 0, False) for p in range(PLANE)], 1
    )
    new_momentum = updated(lay, proj_basis, panel, momentum, tokens * lay.replicas)
    y0, y1, early = [first[:, i * width:(i + 1) * width] for i in range(3)]
    late, early_other, late_other = [second[:, i * width:(i + 1) * width] for i in range(3)]

    z1 = end_swap(y1)
    z3 = mid_swap(early)
    z2 = lay.levels(early, 2, (0, 3))
    late, early_other = after((late, early_other), z1, z2, z3)
    z2b = mid_swap(early_other)
    z_late = lay.levels(jnp.concatenate([late, late_other], 1), 2, (1, 2))
    z3b = lay.levels(late, 3, (0, 3))
    add = lambda *xs: sum(x.astype(f32) for x in xs).astype(bf16)
    z2 = add(z2, z2b, z_late[:, :width])
    z3 = add(z3, z3b, z_late[:, width:])
    input_grad = jnp.concatenate(
        [
            jnp.where(
                level == b,
                y0,
                jnp.where(level == b ^ 1, z1, jnp.where(level == b ^ 2, z2, z3)),
            )
            for b in range(lay.line)
        ],
        1,
    )
    return input_grad, new_momentum


def solution(mesh):
    placed = (
        P(("dp", "tensor"), None),
        P("dp", "tensor"),
        P("dp", "tensor"),
        P(),
        P("dp", "tensor"),
    )
    four = mesh.shape["dp"] == 4 * PLANE and mesh.shape["tensor"] == 2
    return jax.shard_map(
        line_of_four if four else long_line,
        mesh=mesh,
        in_specs=placed,
        out_specs=(P(("dp", "tensor"), None), P("dp", "tensor")),
        check_vma=False,
    )
```

```python
import math

import jax
import jax.numpy as jnp
from jax import lax
from jax.experimental import pallas as pl
from jax.experimental.pallas import tpu as pltpu
from jax.sharding import PartitionSpec as P

momentum_decay = 0.9
PLANE = 4
f32, bf16 = jnp.float32, jnp.bfloat16


def after(x, *first):
    return lax.optimization_barrier((x, first))[0]


def nt(a, b):
    return lax.dot_general(a, b, (((1,), (1,)), ((), ())), preferred_element_type=f32)


def tn(a, b):
    return lax.dot_general(a, b, (((0,), (0,)), ((), ())), preferred_element_type=f32)


class Layout:
    def __init__(self):
        self.replicas, self.cores = lax.axis_size("dp"), lax.axis_size("tensor")
        self.line = self.replicas // PLANE
        self.me, self.core = lax.axis_index("dp"), lax.axis_index("tensor")
        self.place, self.level = self.me % PLANE, self.me // PLANE

    def across(self, x, r):
        return lax.ppermute(x, "dp", [(d, d ^ r) for d in range(self.replicas)])

    def levels(self, x, s, only=None):
        pairs = [
            (d, d ^ (s * PLANE)) for d in range(self.replicas) if only is None or d // PLANE in only
        ]
        return lax.ppermute(x, "dp", pairs)

    def cut(self, x, r):
        quarter = x.shape[1] // PLANE
        return lax.dynamic_slice_in_dim(x, (self.place ^ r) * quarter, quarter, 1)

    def in_order(self, parts, axis):
        size = parts[0].shape[axis]
        shape = list(parts[0].shape)
        shape[axis] *= PLANE
        whole = jnp.zeros(shape, parts[0].dtype)
        for r, part in enumerate(parts):
            whole = lax.dynamic_update_slice_in_dim(whole, part, (self.place ^ r) * size, axis)
        return whole

    def core_sum(self, part, lines):
        width = part.shape[1]
        if self.cores == 2:
            part = part.reshape(lines, 2, -1, width)
            keep = lax.dynamic_index_in_dim(part, self.core, 1, False)
            give = lax.dynamic_index_in_dim(part, 1 - self.core, 1, False)
            got = lax.ppermute(give, "tensor", [(0, 1), (1, 0)])
            return (keep.astype(f32) + got.astype(f32)).astype(bf16)
        return lax.psum_scatter(
            part.reshape(lines, -1, width), "tensor", scatter_dimension=1, tiled=True
        )


def projected(lay, inputs, proj_basis):
    proj = jnp.dot(inputs.astype(f32), proj_basis, precision=lax.Precision.HIGHEST).astype(bf16)
    proj = lax.all_gather(proj, "tensor", axis=0, tiled=True)
    return [proj] + [lay.across(proj, r) for r in range(1, PLANE)]


def panel_shares(lay, plane_proj, pieces):
    panel = sum(tn(q, a) for q, a in zip(plane_proj, pieces))
    share = panel.shape[0] // lay.line
    share_of = lambda x, s: lax.dynamic_slice_in_dim(x, (lay.level ^ s) * share, share, 0)
    half = panel.astype(bf16)
    return [share_of(panel, 0)] + [lay.levels(share_of(half, s), s) for s in range(1, lay.line)]


def panel_quarter(lay, shares):
    summed = sum(x.astype(f32) for x in shares).astype(bf16)
    share, quarter = summed.shape
    panel_q = jnp.zeros((share * lay.line, quarter), bf16)
    for s in range(lay.line):
        got = lay.levels(summed, s) if s else summed
        panel_q = lax.dynamic_update_slice_in_dim(panel_q, got, (lay.level ^ s) * share, 0)
    return panel_q


def panel_whole(lay, panel_q):
    return lay.in_order([panel_q] + [lay.across(panel_q, r) for r in range(1, PLANE)], 1)


def updated(lay, proj_basis, panel, momentum, tokens):
    rows, rank = momentum.shape[0], proj_basis.shape[1]
    basis_rows = lax.dynamic_slice_in_dim(proj_basis, lay.me * rows, rows, 0)
    scale = math.sqrt(proj_basis.shape[0] / rank) / math.sqrt(tokens)
    update = jnp.dot(basis_rows.astype(bf16), panel, preferred_element_type=f32)
    return momentum_decay * momentum + update * scale


def long_line(inputs, out_grad, weight, proj_basis, momentum):
    lay = Layout()
    line, level, cores = lay.line, lay.level, lay.cores
    tokens = out_grad.shape[0]
    pieces = [lay.cut(out_grad, 0)] + [lay.across(lay.cut(out_grad, r), r) for r in range(1, PLANE)]
    weights = [lay.cut(weight, 0)] + [lay.across(lay.cut(weight, r), r) for r in range(1, PLANE)]
    groups = [[p + PLANE * z for z in range(line)] for p in range(PLANE)]
    shares = panel_shares(lay, projected(lay, inputs, proj_basis), pieces)
    panel = panel_whole(lay, panel_quarter(lay, shares))
    new_momentum = updated(lay, proj_basis, panel, momentum, tokens * lay.replicas)
    held = lay.in_order(weights, 0)
    width = held.shape[0]
    total = 0.0
    for r, piece in enumerate(pieces):
        block = lax.all_gather(piece, "dp", axis_index_groups=groups, axis=0, tiled=True)
        part = lay.core_sum(nt(block, held).astype(bf16), line)
        total = total + (lay.across(part, r) if r else part).astype(f32)
    total = total.astype(bf16)
    input_grad = jnp.zeros((tokens // cores, line * width), bf16)
    for s in range(line):
        got = lax.dynamic_index_in_dim(total, level ^ s, 0, False)
        got = lay.levels(got, s) if s else got
        input_grad = lax.dynamic_update_slice_in_dim(input_grad, got, (level ^ s) * width, 1)
    return input_grad, new_momentum


def products(lay, sources, buffers, fills, jobs, width):
    scalars = jnp.stack([lay.place, lay.core]).astype(jnp.int32)
    block = buffers[jobs[0][0]][0]
    half = block // PLANE // 2
    piece = width // PLANE

    def kernel(scalar_ref, *refs):
        ins, refs = refs[: len(sources)], refs[len(sources):]
        keep_ref, give_ref, *scratch = refs
        buffer_refs, sems = scratch[:-1], scratch[-1]
        place, core = scalar_ref[0], scalar_ref[1]
        copies = []
        for i, (s, c0, b, r0, c1, cols) in enumerate(fills):
            n = sources[s].shape[0]
            copies.append(
                pltpu.make_async_copy(
                    ins[s].at[:, pl.ds(c0, cols)],
                    buffer_refs[b].at[pl.ds(r0, n), pl.ds(c1, cols)],
                    sems.at[i],
                )
            )
        for copy in copies:
            copy.start()
        waited = set()

        def need(ids):
            for i in ids:
                if i not in waited:
                    copies[i].wait()
                    waited.add(i)

        for at, (a, b, a0, b0, cols, a_ids, b_ids) in enumerate(jobs):
            need(a_ids)
            for r in range(PLANE):
                need(b_ids(r))
                column = at * width + pl.multiple_of((place ^ r) * piece, piece)
                for p in range(0, PLANE, 2):
                    x = nt(
                        buffer_refs[a][2 * p * half:(2 * p + 4) * half, a0:a0 + cols],
                        buffer_refs[b][r * piece:(r + 1) * piece, b0:b0 + cols],
                    ).astype(bf16)
                    for i in range(2):
                        low, high = x[2 * i * half:][:half], x[(2 * i + 1) * half:][:half]
                        keep_ref[p + i, :, pl.ds(column, piece)] = jnp.where(core == 0, low, high)
                        give_ref[p + i, :, pl.ds(column, piece)] = jnp.where(core == 0, high, low)
        need(range(len(copies)))

    out = jax.ShapeDtypeStruct((PLANE, half, len(jobs) * width), bf16)
    return pl.pallas_call(
        kernel,
        out_shape=(out, out),
        in_specs=[pl.BlockSpec(memory_space=pltpu.SMEM)]
        + [pl.BlockSpec(memory_space=pl.ANY)] * len(sources),
        out_specs=[pl.BlockSpec(memory_space=pltpu.VMEM)] * 2,
        scratch_shapes=[pltpu.VMEM(shape, bf16) for shape in buffers]
        + [pltpu.SemaphoreType.DMA((len(fills),))],
        compiler_params=pltpu.CompilerParams(vmem_limit_bytes=36 * 2**20),
        cost_estimate=pl.CostEstimate(flops=10**6, bytes_accessed=10**5, transcendentals=0),
    )(scalars, *sources)


def line_of_four(inputs, out_grad, weight, proj_basis, momentum):
    lay = Layout()
    level, across = lay.level, lay.across
    inner = (level == 1) | (level == 2)
    tokens, hidden = out_grad.shape
    rows = weight.shape[0]
    width, block = rows * PLANE, tokens * PLANE
    both = hidden // PLANE
    half = both // 2
    low, high = slice(0, half), slice(half, both)
    end_swap = lambda x: lay.levels(x, 1)
    mid_swap = lambda x: lay.levels(x, 3, (1, 2))
    swap = lambda x: lax.ppermute(x, "tensor", [(0, 1), (1, 0)])
    send = lambda a, w: jnp.where(inner, a, w)

    cuts = [lay.cut(out_grad, r) for r in range(PLANE)]
    plane = [across(cuts[r], r) for r in (1, 2)]
    e0, m0 = end_swap(cuts[0]), mid_swap(cuts[0])
    plane.append(across(after(cuts[3], *plane), 3))
    weight = after(weight, e0, m0)
    parts = [lay.cut(weight, r) for r in range(PLANE)]
    sides = after(jnp.concatenate(plane[:2], 0), e0, m0)
    e1, m1 = end_swap(sides), mid_swap(sides)
    e2, m2 = end_swap(plane[2]), mid_swap(plane[2])
    parts[1:3] = [across(after(parts[r], *plane), r) for r in (1, 2)]
    parts[3] = across(after(parts[3], *parts[1:3]), 3)
    joined = lambda x, c: jnp.concatenate([y[:, c] for y in x], 0)
    near_e, near_m = [e0, after(e1, m2), e2], [m0, m1, m2]
    e_high = joined(near_e, high)
    m_low = joined(near_m, low)
    far0 = mid_swap(joined(near_e, low))
    got_a = send(m_low, jnp.concatenate([w[:, high] for w in parts[:2]], 0))
    got_a = end_swap(got_a)
    proj = projected(lay, after(inputs, e1, m1), proj_basis)
    far1, got = [], []
    for i, w in enumerate(parts[2:]):
        rows_i = slice(i * 2 * tokens, (i + 1) * 2 * tokens)
        far1.append(mid_swap(after(e_high[rows_i], far0, got_a)))
        got.append(end_swap(after(send(far0[rows_i], w[:, high]), got_a, parts[3], *proj)))

    weight_fills = lambda first, b: [(first + r, 0, b, r * rows, 0, both) for r in range(PLANE)]
    none = lambda r: ()
    early0 = send(m_low, got_a)
    own = [after(cuts[0], far0), sides, plane[2]]
    sources = [*own, *near_e, early0, *near_m, *parts]
    starts = (0, tokens, 3 * tokens)
    fills = [(i, 0, 0, row, 0, both) for i, row in enumerate(starts)] + weight_fills(10, 3)
    fills += [(3 + i, 0, 1, row, 0, both) for i, row in enumerate(starts)]
    fills += [(6, 0, 2, 0, 0, half)]
    fills += [(7 + i, half, 2, row, half, half) for i, row in enumerate(starts)]
    jobs = [
        (0, 3, 0, 0, both, (0, 1, 2), lambda r: (3 + r,)),
        (1, 3, 0, 0, both, (7, 8, 9), none),
        (2, 3, 0, 0, both, (10, 11, 12, 13), none),
    ]
    keep, give = products(lay, sources, [(block, both)] * 3 + [(width, both)], fills, jobs, width)
    give = after(give, far1[0], got[0])
    first = (keep.astype(f32) + swap(give).astype(f32)).astype(bf16)
    first_x, first_y = across(first[1], 1), across(first[2], 2)

    panel = sum(tn(q, a) for q, a in zip(proj, [after(cuts[0], give), *plane]))
    panel = panel + end_swap(after(panel.astype(bf16), first)).astype(f32)

    late0 = send(far0, jnp.concatenate(got, 0))
    sources = [after(late0, first), *far1, *near_m, *parts, got_a, *got]
    fills = [(0, 0, 0, 0, 0, half)]
    fills += [(1 + i, 0, 0, 2 * i * tokens, half, half) for i in range(2)] + weight_fills(6, 2)
    fills += [(3 + i, half, 1, row, 0, half) for i, row in enumerate(starts)]
    fills += [(10, 0, 3, 0, 0, half), (11, 0, 3, 2 * rows, 0, half), (12, 0, 3, 3 * rows, 0, half)]
    jobs = [
        (0, 2, 0, 0, both, (0, 1, 2), lambda r: (3 + r,)),
        (1, 3, 0, 0, half, (7, 8, 9), lambda r: ((10,), (), (11,), (12,))[r]),
        (0, 3, half, 0, half, (), none),
    ]
    buffers = [(block, both), (block, half), (width, both), (width, half)]
    keep, give = products(lay, sources, buffers, fills, jobs, width)

    def plane_sum(own, *others):
        return sum(x.astype(f32) for x in (own, *others)).astype(bf16)

    first = plane_sum(first[0], first_x, first_y, across(first[3], 3))
    give = after(give, first)
    second = (keep.astype(f32) + swap(give).astype(f32)).astype(bf16)
    second = plane_sum(second[0], *[across(second[r], r) for r in range(1, PLANE)])
    panel = (panel + lay.levels(after(panel.astype(bf16), second), 2).astype(f32)).astype(bf16)
    panel = jnp.stack([panel] + [across(panel, r) for r in range(1, PLANE)])
    panel = jnp.concatenate(
        [lax.dynamic_index_in_dim(panel, lay.place ^ p, 0, False) for p in range(PLANE)], 1
    )
    new_momentum = updated(lay, proj_basis, panel, momentum, tokens * lay.replicas)
    y0, y1, early = [first[:, i * width:(i + 1) * width] for i in range(3)]
    late, early_other, late_other = [second[:, i * width:(i + 1) * width] for i in range(3)]

    z1 = end_swap(y1)
    z3 = mid_swap(early)
    z2 = lay.levels(early, 2, (0, 3))
    late, early_other = after((late, early_other), z1, z2, z3)
    z2b = mid_swap(early_other)
    z_late = lay.levels(jnp.concatenate([late, late_other], 1), 2, (1, 2))
    z3b = lay.levels(late, 3, (0, 3))
    add = lambda *xs: sum(x.astype(f32) for x in xs).astype(bf16)
    z2 = add(z2, z2b, z_late[:, :width])
    z3 = add(z3, z3b, z_late[:, width:])
    input_grad = jnp.concatenate(
        [
            jnp.where(
                level == b,
                y0,
                jnp.where(level == b ^ 1, z1, jnp.where(level == b ^ 2, z2, z3)),
            )
            for b in range(lay.line)
        ],
        1,
    )
    return input_grad, new_momentum


def solution(mesh):
    placed = (
        P(("dp", "tensor"), None),
        P("dp", "tensor"),
        P("dp", "tensor"),
        P(),
        P("dp", "tensor"),
    )
    four = mesh.shape["dp"] == 4 * PLANE and mesh.shape["tensor"] == 2
    return jax.shard_map(
        line_of_four if four else long_line,
        mesh=mesh,
        in_specs=placed,
        out_specs=(P(("dp", "tensor"), None), P("dp", "tensor")),
        check_vma=False,
    )
```

```python
import math

import jax
import jax.numpy as jnp
from jax import lax
from jax.experimental import pallas as pl
from jax.experimental.pallas import tpu as pltpu
from jax.sharding import PartitionSpec as P

momentum_decay = 0.9
PLANE = 4
f32, bf16 = jnp.float32, jnp.bfloat16


def after(x, *first):
    return lax.optimization_barrier((x, first))[0]


def nt(a, b):
    return lax.dot_general(a, b, (((1,), (1,)), ((), ())), preferred_element_type=f32)


def tn(a, b):
    return lax.dot_general(a, b, (((0,), (0,)), ((), ())), preferred_element_type=f32)


class Layout:
    def __init__(self):
        self.replicas, self.cores = lax.axis_size("dp"), lax.axis_size("tensor")
        self.line = self.replicas // PLANE
        self.me, self.core = lax.axis_index("dp"), lax.axis_index("tensor")
        self.place, self.level = self.me % PLANE, self.me // PLANE

    def across(self, x, r):
        return lax.ppermute(x, "dp", [(d, d ^ r) for d in range(self.replicas)])

    def levels(self, x, s, only=None):
        pairs = [
            (d, d ^ (s * PLANE)) for d in range(self.replicas) if only is None or d // PLANE in only
        ]
        return lax.ppermute(x, "dp", pairs)

    def cut(self, x, r):
        quarter = x.shape[1] // PLANE
        return lax.dynamic_slice_in_dim(x, (self.place ^ r) * quarter, quarter, 1)

    def in_order(self, parts, axis):
        size = parts[0].shape[axis]
        shape = list(parts[0].shape)
        shape[axis] *= PLANE
        whole = jnp.zeros(shape, parts[0].dtype)
        for r, part in enumerate(parts):
            whole = lax.dynamic_update_slice_in_dim(whole, part, (self.place ^ r) * size, axis)
        return whole

    def core_sum(self, part, lines):
        width = part.shape[1]
        if self.cores == 2:
            part = part.reshape(lines, 2, -1, width)
            keep = lax.dynamic_index_in_dim(part, self.core, 1, False)
            give = lax.dynamic_index_in_dim(part, 1 - self.core, 1, False)
            got = lax.ppermute(give, "tensor", [(0, 1), (1, 0)])
            return (keep.astype(f32) + got.astype(f32)).astype(bf16)
        return lax.psum_scatter(
            part.reshape(lines, -1, width), "tensor", scatter_dimension=1, tiled=True
        )


def projected(lay, inputs, proj_basis):
    proj = jnp.dot(inputs.astype(f32), proj_basis, precision=lax.Precision.HIGHEST).astype(bf16)
    proj = lax.all_gather(proj, "tensor", axis=0, tiled=True)
    return [proj] + [lay.across(proj, r) for r in range(1, PLANE)]


def panel_shares(lay, plane_proj, pieces):
    panel = sum(tn(q, a) for q, a in zip(plane_proj, pieces))
    share = panel.shape[0] // lay.line
    share_of = lambda x, s: lax.dynamic_slice_in_dim(x, (lay.level ^ s) * share, share, 0)
    half = panel.astype(bf16)
    return [share_of(panel, 0)] + [lay.levels(share_of(half, s), s) for s in range(1, lay.line)]


def panel_quarter(lay, shares):
    summed = sum(x.astype(f32) for x in shares).astype(bf16)
    share, quarter = summed.shape
    panel_q = jnp.zeros((share * lay.line, quarter), bf16)
    for s in range(lay.line):
        got = lay.levels(summed, s) if s else summed
        panel_q = lax.dynamic_update_slice_in_dim(panel_q, got, (lay.level ^ s) * share, 0)
    return panel_q


def panel_whole(lay, panel_q):
    return lay.in_order([panel_q] + [lay.across(panel_q, r) for r in range(1, PLANE)], 1)


def updated(lay, proj_basis, panel, momentum, tokens):
    rows, rank = momentum.shape[0], proj_basis.shape[1]
    basis_rows = lax.dynamic_slice_in_dim(proj_basis, lay.me * rows, rows, 0)
    scale = math.sqrt(proj_basis.shape[0] / rank) / math.sqrt(tokens)
    update = jnp.dot(basis_rows.astype(bf16), panel, preferred_element_type=f32)
    return momentum_decay * momentum + update * scale


def long_line(inputs, out_grad, weight, proj_basis, momentum):
    lay = Layout()
    line, level, cores = lay.line, lay.level, lay.cores
    tokens = out_grad.shape[0]
    pieces = [lay.cut(out_grad, 0)] + [lay.across(lay.cut(out_grad, r), r) for r in range(1, PLANE)]
    weights = [lay.cut(weight, 0)] + [lay.across(lay.cut(weight, r), r) for r in range(1, PLANE)]
    groups = [[p + PLANE * z for z in range(line)] for p in range(PLANE)]
    shares = panel_shares(lay, projected(lay, inputs, proj_basis), pieces)
    panel = panel_whole(lay, panel_quarter(lay, shares))
    new_momentum = updated(lay, proj_basis, panel, momentum, tokens * lay.replicas)
    held = lay.in_order(weights, 0)
    width = held.shape[0]
    total = 0.0
    for r, piece in enumerate(pieces):
        block = lax.all_gather(piece, "dp", axis_index_groups=groups, axis=0, tiled=True)
        part = lay.core_sum(nt(block, held).astype(bf16), line)
        total = total + (lay.across(part, r) if r else part).astype(f32)
    total = total.astype(bf16)
    input_grad = jnp.zeros((tokens // cores, line * width), bf16)
    for s in range(line):
        got = lax.dynamic_index_in_dim(total, level ^ s, 0, False)
        got = lay.levels(got, s) if s else got
        input_grad = lax.dynamic_update_slice_in_dim(input_grad, got, (level ^ s) * width, 1)
    return input_grad, new_momentum


def products(lay, sources, buffers, fills, jobs, width):
    scalars = jnp.stack([lay.place, lay.core]).astype(jnp.int32)
    block = buffers[jobs[0][0]][0]
    half = block // PLANE // 2
    piece = width // PLANE

    def kernel(scalar_ref, *refs):
        ins, refs = refs[: len(sources)], refs[len(sources):]
        keep_ref, give_ref, *scratch = refs
        buffer_refs, sems = scratch[:-1], scratch[-1]
        place, core = scalar_ref[0], scalar_ref[1]
        copies = []
        for i, (s, c0, b, r0, c1, cols) in enumerate(fills):
            n = sources[s].shape[0]
            copies.append(
                pltpu.make_async_copy(
                    ins[s].at[:, pl.ds(c0, cols)],
                    buffer_refs[b].at[pl.ds(r0, n), pl.ds(c1, cols)],
                    sems.at[i],
                )
            )
        for copy in copies:
            copy.start()
        waited = set()

        def need(ids):
            for i in ids:
                if i not in waited:
                    copies[i].wait()
                    waited.add(i)

        for at, (a, b, a0, b0, cols, a_ids, b_ids) in enumerate(jobs):
            need(a_ids)
            for r in range(PLANE):
                need(b_ids(r))
                column = at * width + pl.multiple_of((place ^ r) * piece, piece)
                for p in range(0, PLANE, 2):
                    x = nt(
                        buffer_refs[a][2 * p * half:(2 * p + 4) * half, a0:a0 + cols],
                        buffer_refs[b][r * piece:(r + 1) * piece, b0:b0 + cols],
                    ).astype(bf16)
                    for i in range(2):
                        low, high = x[2 * i * half:][:half], x[(2 * i + 1) * half:][:half]
                        keep_ref[p + i, :, pl.ds(column, piece)] = jnp.where(core == 0, low, high)
                        give_ref[p + i, :, pl.ds(column, piece)] = jnp.where(core == 0, high, low)
        need(range(len(copies)))

    out = jax.ShapeDtypeStruct((PLANE, half, len(jobs) * width), bf16)
    return pl.pallas_call(
        kernel,
        out_shape=(out, out),
        in_specs=[pl.BlockSpec(memory_space=pltpu.SMEM)]
        + [pl.BlockSpec(memory_space=pl.ANY)] * len(sources),
        out_specs=[pl.BlockSpec(memory_space=pltpu.VMEM)] * 2,
        scratch_shapes=[pltpu.VMEM(shape, bf16) for shape in buffers]
        + [pltpu.SemaphoreType.DMA((len(fills),))],
        compiler_params=pltpu.CompilerParams(vmem_limit_bytes=36 * 2**20),
        cost_estimate=pl.CostEstimate(flops=10**6, bytes_accessed=10**5, transcendentals=0),
    )(scalars, *sources)


def line_of_four(inputs, out_grad, weight, proj_basis, momentum):
    lay = Layout()
    level, across = lay.level, lay.across
    inner = (level == 1) | (level == 2)
    tokens, hidden = out_grad.shape
    rows = weight.shape[0]
    width, block = rows * PLANE, tokens * PLANE
    both = hidden // PLANE
    half = both // 2
    low, high = slice(0, half), slice(half, both)
    end_swap = lambda x: lay.levels(x, 1)
    mid_swap = lambda x: lay.levels(x, 3, (1, 2))
    swap = lambda x: lax.ppermute(x, "tensor", [(0, 1), (1, 0)])
    send = lambda a, w: jnp.where(inner, a, w)

    cuts = [lay.cut(out_grad, r) for r in range(PLANE)]
    plane = [across(cuts[r], r) for r in (1, 2)]
    e0, m0 = end_swap(cuts[0]), mid_swap(cuts[0])
    plane.append(across(after(cuts[3], *plane), 3))
    weight = after(weight, e0, m0)
    parts = [lay.cut(weight, r) for r in range(PLANE)]
    sides = after(jnp.concatenate(plane[:2], 0), e0, m0)
    e1, m1 = end_swap(sides), mid_swap(sides)
    e2, m2 = end_swap(plane[2]), mid_swap(plane[2])
    proj = projected(lay, after(inputs, plane[0]), proj_basis)
    parts[1:3] = [across(after(parts[r], *plane, *proj), r) for r in (1, 2)]
    parts[3] = across(after(parts[3], *parts[1:3]), 3)
    joined = lambda x, c: jnp.concatenate([y[:, c] for y in x], 0)
    near_e, near_m = [e0, after(e1, m2), e2], [m0, m1, m2]
    e_high = joined(near_e, high)
    m_low = joined(near_m, low)
    panel = sum(tn(q, a) for q, a in zip(proj, [cuts[0], *plane]))
    far0 = mid_swap(after(joined(near_e, low), panel))
    panel = panel + end_swap(panel.astype(bf16)).astype(f32)
    got_a = send(m_low, jnp.concatenate([w[:, high] for w in parts[:2]], 0))
    got_a = end_swap(after(got_a, panel))
    panel = (panel + lay.levels(panel.astype(bf16), 2).astype(f32)).astype(bf16)
    far1, got = [], []
    for i, w in enumerate(parts[2:]):
        rows_i = slice(i * 2 * tokens, (i + 1) * 2 * tokens)
        far1.append(mid_swap(after(e_high[rows_i], far0, got_a)))
        got.append(end_swap(after(send(far0[rows_i], w[:, high]), got_a, parts[3], panel)))

    weight_fills = lambda first, b: [(first + r, 0, b, r * rows, 0, both) for r in range(PLANE)]
    none = lambda r: ()
    early0 = send(m_low, got_a)
    own = [after(cuts[0], far0), sides, plane[2]]
    sources = [*own, *near_e, early0, *near_m, *parts]
    starts = (0, tokens, 3 * tokens)
    fills = [(i, 0, 0, row, 0, both) for i, row in enumerate(starts)] + weight_fills(10, 3)
    fills += [(3 + i, 0, 1, row, 0, both) for i, row in enumerate(starts)]
    fills += [(6, 0, 2, 0, 0, half)]
    fills += [(7 + i, half, 2, row, half, half) for i, row in enumerate(starts)]
    jobs = [
        (0, 3, 0, 0, both, (0, 1, 2), lambda r: (3 + r,)),
        (1, 3, 0, 0, both, (7, 8, 9), none),
        (2, 3, 0, 0, both, (10, 11, 12, 13), none),
    ]
    keep, give = products(lay, sources, [(block, both)] * 3 + [(width, both)], fills, jobs, width)
    give = after(give, far1[0], got[0])
    first = (keep.astype(f32) + swap(give).astype(f32)).astype(bf16)
    first_x, first_y = across(first[1], 1), across(first[2], 2)

    late0 = send(far0, jnp.concatenate(got, 0))
    sources = [after(late0, first), *far1, *near_m, *parts, got_a, *got]
    fills = [(0, 0, 0, 0, 0, half)]
    fills += [(1 + i, 0, 0, 2 * i * tokens, half, half) for i in range(2)] + weight_fills(6, 2)
    fills += [(3 + i, half, 1, row, 0, half) for i, row in enumerate(starts)]
    fills += [(10, 0, 3, 0, 0, half), (11, 0, 3, 2 * rows, 0, half), (12, 0, 3, 3 * rows, 0, half)]
    jobs = [
        (0, 2, 0, 0, both, (0, 1, 2), lambda r: (3 + r,)),
        (1, 3, 0, 0, half, (7, 8, 9), lambda r: ((10,), (), (11,), (12,))[r]),
        (0, 3, half, 0, half, (), none),
    ]
    buffers = [(block, both), (block, half), (width, both), (width, half)]
    keep, give = products(lay, sources, buffers, fills, jobs, width)

    def plane_sum(own, *others):
        return sum(x.astype(f32) for x in (own, *others)).astype(bf16)

    first = plane_sum(first[0], first_x, first_y, across(first[3], 3))
    give = after(give, first)
    second = (keep.astype(f32) + swap(give).astype(f32)).astype(bf16)
    second = plane_sum(second[0], *[across(second[r], r) for r in range(1, PLANE)])
    panel = after(panel, second)
    panel = jnp.stack([panel] + [across(panel, r) for r in range(1, PLANE)])
    panel = jnp.concatenate(
        [lax.dynamic_index_in_dim(panel, lay.place ^ p, 0, False) for p in range(PLANE)], 1
    )
    new_momentum = updated(lay, proj_basis, panel, momentum, tokens * lay.replicas)
    y0, y1, early = [first[:, i * width:(i + 1) * width] for i in range(3)]
    late, early_other, late_other = [second[:, i * width:(i + 1) * width] for i in range(3)]

    z1 = end_swap(y1)
    z3 = mid_swap(early)
    z2 = lay.levels(early, 2, (0, 3))
    late, early_other = after((late, early_other), z1, z2, z3)
    z2b = mid_swap(early_other)
    z_late = lay.levels(jnp.concatenate([late, late_other], 1), 2, (1, 2))
    z3b = lay.levels(late, 3, (0, 3))
    add = lambda *xs: sum(x.astype(f32) for x in xs).astype(bf16)
    z2 = add(z2, z2b, z_late[:, :width])
    z3 = add(z3, z3b, z_late[:, width:])
    input_grad = jnp.concatenate(
        [
            jnp.where(
                level == b,
                y0,
                jnp.where(level == b ^ 1, z1, jnp.where(level == b ^ 2, z2, z3)),
            )
            for b in range(lay.line)
        ],
        1,
    )
    return input_grad, new_momentum


def solution(mesh):
    placed = (
        P(("dp", "tensor"), None),
        P("dp", "tensor"),
        P("dp", "tensor"),
        P(),
        P("dp", "tensor"),
    )
    four = mesh.shape["dp"] == 4 * PLANE and mesh.shape["tensor"] == 2
    return jax.shard_map(
        line_of_four if four else long_line,
        mesh=mesh,
        in_specs=placed,
        out_specs=(P(("dp", "tensor"), None), P("dp", "tensor")),
        check_vma=False,
    )
```

```python
import math

import jax
import jax.numpy as jnp
from jax import lax
from jax.experimental import pallas as pl
from jax.experimental.pallas import tpu as pltpu
from jax.sharding import PartitionSpec as P

momentum_decay = 0.9
PLANE = 4
f32, bf16 = jnp.float32, jnp.bfloat16


def after(x, *first):
    return lax.optimization_barrier((x, first))[0]


def nt(a, b):
    return lax.dot_general(a, b, (((1,), (1,)), ((), ())), preferred_element_type=f32)


def tn(a, b):
    return lax.dot_general(a, b, (((0,), (0,)), ((), ())), preferred_element_type=f32)


class Layout:
    def __init__(self):
        self.replicas, self.cores = lax.axis_size("dp"), lax.axis_size("tensor")
        self.line = self.replicas // PLANE
        self.me, self.core = lax.axis_index("dp"), lax.axis_index("tensor")
        self.place, self.level = self.me % PLANE, self.me // PLANE

    def across(self, x, r):
        return lax.ppermute(x, "dp", [(d, d ^ r) for d in range(self.replicas)])

    def levels(self, x, s, only=None):
        pairs = [
            (d, d ^ (s * PLANE)) for d in range(self.replicas) if only is None or d // PLANE in only
        ]
        return lax.ppermute(x, "dp", pairs)

    def cut(self, x, r):
        quarter = x.shape[1] // PLANE
        return lax.dynamic_slice_in_dim(x, (self.place ^ r) * quarter, quarter, 1)

    def in_order(self, parts, axis):
        size = parts[0].shape[axis]
        shape = list(parts[0].shape)
        shape[axis] *= PLANE
        whole = jnp.zeros(shape, parts[0].dtype)
        for r, part in enumerate(parts):
            whole = lax.dynamic_update_slice_in_dim(whole, part, (self.place ^ r) * size, axis)
        return whole

    def core_sum(self, part, lines):
        width = part.shape[1]
        if self.cores == 2:
            part = part.reshape(lines, 2, -1, width)
            keep = lax.dynamic_index_in_dim(part, self.core, 1, False)
            give = lax.dynamic_index_in_dim(part, 1 - self.core, 1, False)
            got = lax.ppermute(give, "tensor", [(0, 1), (1, 0)])
            return (keep.astype(f32) + got.astype(f32)).astype(bf16)
        return lax.psum_scatter(
            part.reshape(lines, -1, width), "tensor", scatter_dimension=1, tiled=True
        )


def projected(lay, inputs, proj_basis):
    proj = jnp.dot(inputs.astype(f32), proj_basis, precision=lax.Precision.HIGHEST).astype(bf16)
    proj = lax.all_gather(proj, "tensor", axis=0, tiled=True)
    return [proj] + [lay.across(proj, r) for r in range(1, PLANE)]


def panel_shares(lay, plane_proj, pieces):
    panel = sum(tn(q, a) for q, a in zip(plane_proj, pieces))
    share = panel.shape[0] // lay.line
    share_of = lambda x, s: lax.dynamic_slice_in_dim(x, (lay.level ^ s) * share, share, 0)
    half = panel.astype(bf16)
    return [share_of(panel, 0)] + [lay.levels(share_of(half, s), s) for s in range(1, lay.line)]


def panel_quarter(lay, shares):
    summed = sum(x.astype(f32) for x in shares).astype(bf16)
    share, quarter = summed.shape
    panel_q = jnp.zeros((share * lay.line, quarter), bf16)
    for s in range(lay.line):
        got = lay.levels(summed, s) if s else summed
        panel_q = lax.dynamic_update_slice_in_dim(panel_q, got, (lay.level ^ s) * share, 0)
    return panel_q


def panel_whole(lay, panel_q):
    return lay.in_order([panel_q] + [lay.across(panel_q, r) for r in range(1, PLANE)], 1)


def updated(lay, proj_basis, panel, momentum, tokens):
    rows, rank = momentum.shape[0], proj_basis.shape[1]
    basis_rows = lax.dynamic_slice_in_dim(proj_basis, lay.me * rows, rows, 0)
    scale = math.sqrt(proj_basis.shape[0] / rank) / math.sqrt(tokens)
    update = jnp.dot(basis_rows.astype(bf16), panel, preferred_element_type=f32)
    return momentum_decay * momentum + update * scale


def long_line(inputs, out_grad, weight, proj_basis, momentum):
    lay = Layout()
    line, level, cores = lay.line, lay.level, lay.cores
    tokens = out_grad.shape[0]
    pieces = [lay.cut(out_grad, 0)] + [lay.across(lay.cut(out_grad, r), r) for r in range(1, PLANE)]
    weights = [lay.cut(weight, 0)] + [lay.across(lay.cut(weight, r), r) for r in range(1, PLANE)]
    groups = [[p + PLANE * z for z in range(line)] for p in range(PLANE)]
    shares = panel_shares(lay, projected(lay, inputs, proj_basis), pieces)
    panel = panel_whole(lay, panel_quarter(lay, shares))
    new_momentum = updated(lay, proj_basis, panel, momentum, tokens * lay.replicas)
    held = lay.in_order(weights, 0)
    width = held.shape[0]
    total = 0.0
    for r, piece in enumerate(pieces):
        block = lax.all_gather(piece, "dp", axis_index_groups=groups, axis=0, tiled=True)
        part = lay.core_sum(nt(block, held).astype(bf16), line)
        total = total + (lay.across(part, r) if r else part).astype(f32)
    total = total.astype(bf16)
    input_grad = jnp.zeros((tokens // cores, line * width), bf16)
    for s in range(line):
        got = lax.dynamic_index_in_dim(total, level ^ s, 0, False)
        got = lay.levels(got, s) if s else got
        input_grad = lax.dynamic_update_slice_in_dim(input_grad, got, (level ^ s) * width, 1)
    return input_grad, new_momentum


def products(lay, sources, buffers, fills, jobs, width):
    scalars = jnp.stack([lay.place, lay.core]).astype(jnp.int32)
    block = buffers[jobs[0][0]][0]
    half = block // PLANE // 2
    piece = width // PLANE

    def kernel(scalar_ref, *refs):
        ins, refs = refs[: len(sources)], refs[len(sources):]
        keep_ref, give_ref, *scratch = refs
        buffer_refs, sems = scratch[:-1], scratch[-1]
        place, core = scalar_ref[0], scalar_ref[1]
        copies = []
        for i, (s, c0, b, r0, c1, cols) in enumerate(fills):
            n = sources[s].shape[0]
            copies.append(
                pltpu.make_async_copy(
                    ins[s].at[:, pl.ds(c0, cols)],
                    buffer_refs[b].at[pl.ds(r0, n), pl.ds(c1, cols)],
                    sems.at[i],
                )
            )
        for copy in copies:
            copy.start()
        waited = set()

        def need(ids):
            for i in ids:
                if i not in waited:
                    copies[i].wait()
                    waited.add(i)

        for at, (a, b, a0, b0, cols, a_ids, b_ids) in enumerate(jobs):
            need(a_ids)
            for r in range(PLANE):
                need(b_ids(r))
                column = at * width + pl.multiple_of((place ^ r) * piece, piece)
                for p in range(0, PLANE, 2):
                    x = nt(
                        buffer_refs[a][2 * p * half:(2 * p + 4) * half, a0:a0 + cols],
                        buffer_refs[b][r * piece:(r + 1) * piece, b0:b0 + cols],
                    ).astype(bf16)
                    for i in range(2):
                        low, high = x[2 * i * half:][:half], x[(2 * i + 1) * half:][:half]
                        keep_ref[p + i, :, pl.ds(column, piece)] = jnp.where(core == 0, low, high)
                        give_ref[p + i, :, pl.ds(column, piece)] = jnp.where(core == 0, high, low)
        need(range(len(copies)))

    out = jax.ShapeDtypeStruct((PLANE, half, len(jobs) * width), bf16)
    return pl.pallas_call(
        kernel,
        out_shape=(out, out),
        in_specs=[pl.BlockSpec(memory_space=pltpu.SMEM)]
        + [pl.BlockSpec(memory_space=pl.ANY)] * len(sources),
        out_specs=[pl.BlockSpec(memory_space=pltpu.VMEM)] * 2,
        scratch_shapes=[pltpu.VMEM(shape, bf16) for shape in buffers]
        + [pltpu.SemaphoreType.DMA((len(fills),))],
        compiler_params=pltpu.CompilerParams(vmem_limit_bytes=36 * 2**20),
        cost_estimate=pl.CostEstimate(flops=10**6, bytes_accessed=10**5, transcendentals=0),
    )(scalars, *sources)


def line_of_four(inputs, out_grad, weight, proj_basis, momentum):
    lay = Layout()
    level, across = lay.level, lay.across
    inner = (level == 1) | (level == 2)
    tokens, hidden = out_grad.shape
    rows = weight.shape[0]
    width, block = rows * PLANE, tokens * PLANE
    both = hidden // PLANE
    half = both // 2
    low, high = slice(0, half), slice(half, both)
    end_swap = lambda x: lay.levels(x, 1)
    mid_swap = lambda x: lay.levels(x, 3, (1, 2))
    swap = lambda x: lax.ppermute(x, "tensor", [(0, 1), (1, 0)])
    send = lambda a, w: jnp.where(inner, a, w)

    cuts = [lay.cut(out_grad, r) for r in range(PLANE)]
    plane = [across(cuts[r], r) for r in (1, 2)]
    e0, m0 = end_swap(cuts[0]), mid_swap(cuts[0])
    plane.append(across(after(cuts[3], *plane), 3))
    weight = after(weight, e0, m0)
    parts = [lay.cut(weight, r) for r in range(PLANE)]
    sides = after(jnp.concatenate(plane[:2], 0), e0, m0)
    e1, m1 = end_swap(sides), mid_swap(sides)
    e2, m2 = end_swap(plane[2]), mid_swap(plane[2])
    parts[1:3] = [across(after(parts[r], *plane), r) for r in (1, 2)]
    parts[3] = across(after(parts[3], *parts[1:3]), 3)
    joined = lambda x, c: jnp.concatenate([y[:, c] for y in x], 0)
    near_e, near_m = [e0, after(e1, m2), e2], [m0, m1, m2]
    e_high = joined(near_e, high)
    m_low = joined(near_m, low)
    far0 = mid_swap(joined(near_e, low))
    got_a = send(m_low, jnp.concatenate([w[:, high] for w in parts[:2]], 0))
    got_a = end_swap(got_a)
    proj = projected(lay, after(inputs, e1, m1), proj_basis)
    far1, got = [], []
    for i, w in enumerate(parts[2:]):
        rows_i = slice(i * 2 * tokens, (i + 1) * 2 * tokens)
        far1.append(mid_swap(after(e_high[rows_i], far0, got_a)))
        got.append(end_swap(after(send(far0[rows_i], w[:, high]), got_a, parts[3], *proj)))

    weight_fills = lambda first, b: [(first + r, 0, b, r * rows, 0, both) for r in range(PLANE)]
    none = lambda r: ()
    early0 = send(m_low, got_a)
    own = [after(cuts[0], far0), sides, plane[2]]
    sources = [*own, *near_e, early0, *near_m, *parts]
    starts = (0, tokens, 3 * tokens)
    fills = [(i, 0, 0, row, 0, both) for i, row in enumerate(starts)] + weight_fills(10, 3)
    fills += [(3 + i, 0, 1, row, 0, both) for i, row in enumerate(starts)]
    fills += [(6, 0, 2, 0, 0, half)]
    fills += [(7 + i, half, 2, row, half, half) for i, row in enumerate(starts)]
    jobs = [
        (0, 3, 0, 0, both, (0, 1, 2), lambda r: (3 + r,)),
        (1, 3, 0, 0, both, (7, 8, 9), none),
        (2, 3, 0, 0, both, (10, 11, 12, 13), none),
    ]
    keep, give = products(lay, sources, [(block, both)] * 3 + [(width, both)], fills, jobs, width)
    give = after(give, far1[0], got[0])
    first = (keep.astype(f32) + swap(give).astype(f32)).astype(bf16)
    first_x, first_y = across(first[1], 1), across(first[2], 2)

    panel = sum(tn(q, a) for q, a in zip(proj, [after(cuts[0], give), *plane]))

    late0 = send(far0, jnp.concatenate(got, 0))
    sources = [after(late0, first), *far1, *near_m, *parts, got_a, *got]
    fills = [(0, 0, 0, 0, 0, half)]
    fills += [(1 + i, 0, 0, 2 * i * tokens, half, half) for i in range(2)] + weight_fills(6, 2)
    fills += [(3 + i, half, 1, row, 0, half) for i, row in enumerate(starts)]
    fills += [(10, 0, 3, 0, 0, half), (11, 0, 3, 2 * rows, 0, half), (12, 0, 3, 3 * rows, 0, half)]
    jobs = [
        (0, 2, 0, 0, both, (0, 1, 2), lambda r: (3 + r,)),
        (1, 3, 0, 0, half, (7, 8, 9), lambda r: ((10,), (), (11,), (12,))[r]),
        (0, 3, half, 0, half, (), none),
    ]
    buffers = [(block, both), (block, half), (width, both), (width, half)]
    keep, give = products(lay, sources, buffers, fills, jobs, width)

    def plane_sum(own, *others):
        return sum(x.astype(f32) for x in (own, *others)).astype(bf16)

    first = plane_sum(first[0], first_x, first_y, across(first[3], 3))
    give = after(give, first)
    second = (keep.astype(f32) + swap(give).astype(f32)).astype(bf16)
    arrived = [across(second[r], r) for r in range(1, PLANE)]
    totals = plane_sum(second[0], *arrived)
    part = panel.astype(bf16)
    panel = panel + sum(lay.levels(part, s).astype(f32) for s in range(1, lay.line))
    panel = panel.astype(bf16)
    y1 = after(first[:, width:2 * width], panel)
    panel = after(panel, totals)
    panel = jnp.stack([panel] + [across(panel, r) for r in range(1, PLANE)])
    panel = jnp.concatenate(
        [lax.dynamic_index_in_dim(panel, lay.place ^ p, 0, False) for p in range(PLANE)], 1
    )
    new_momentum = updated(lay, proj_basis, panel, momentum, tokens * lay.replicas)
    y0, early = first[:, :width], first[:, 2 * width:]
    second = totals
    late, early_other, late_other = [second[:, i * width:(i + 1) * width] for i in range(3)]

    z1 = end_swap(y1)
    z3 = mid_swap(early)
    z2 = lay.levels(early, 2, (0, 3))
    late, early_other = after((late, early_other), z1, z2, z3)
    z2b = mid_swap(early_other)
    z_late = lay.levels(jnp.concatenate([late, late_other], 1), 2, (1, 2))
    z3b = lay.levels(late, 3, (0, 3))
    add = lambda *xs: sum(x.astype(f32) for x in xs).astype(bf16)
    z2 = add(z2, z2b, z_late[:, :width])
    z3 = add(z3, z3b, z_late[:, width:])
    input_grad = jnp.concatenate(
        [
            jnp.where(
                level == b,
                y0,
                jnp.where(level == b ^ 1, z1, jnp.where(level == b ^ 2, z2, z3)),
            )
            for b in range(lay.line)
        ],
        1,
    )
    return input_grad, new_momentum


def solution(mesh):
    placed = (
        P(("dp", "tensor"), None),
        P("dp", "tensor"),
        P("dp", "tensor"),
        P(),
        P("dp", "tensor"),
    )
    four = mesh.shape["dp"] == 4 * PLANE and mesh.shape["tensor"] == 2
    return jax.shard_map(
        line_of_four if four else long_line,
        mesh=mesh,
        in_specs=placed,
        out_specs=(P(("dp", "tensor"), None), P("dp", "tensor")),
        check_vma=False,
    )
```

```python
import math

import jax
import jax.numpy as jnp
from jax import lax
from jax.experimental import pallas as pl
from jax.experimental.pallas import tpu as pltpu
from jax.sharding import PartitionSpec as P

momentum_decay = 0.9
PLANE = 4
f32, bf16 = jnp.float32, jnp.bfloat16


def after(x, *first):
    return lax.optimization_barrier((x, first))[0]


def nt(a, b):
    return lax.dot_general(a, b, (((1,), (1,)), ((), ())), preferred_element_type=f32)


def tn(a, b):
    return lax.dot_general(a, b, (((0,), (0,)), ((), ())), preferred_element_type=f32)


class Layout:
    def __init__(self):
        self.replicas, self.cores = lax.axis_size("dp"), lax.axis_size("tensor")
        self.line = self.replicas // PLANE
        self.me, self.core = lax.axis_index("dp"), lax.axis_index("tensor")
        self.place, self.level = self.me % PLANE, self.me // PLANE

    def across(self, x, r):
        return lax.ppermute(x, "dp", [(d, d ^ r) for d in range(self.replicas)])

    def levels(self, x, s, only=None):
        pairs = [
            (d, d ^ (s * PLANE)) for d in range(self.replicas) if only is None or d // PLANE in only
        ]
        return lax.ppermute(x, "dp", pairs)

    def cut(self, x, r):
        quarter = x.shape[1] // PLANE
        return lax.dynamic_slice_in_dim(x, (self.place ^ r) * quarter, quarter, 1)

    def in_order(self, parts, axis):
        size = parts[0].shape[axis]
        shape = list(parts[0].shape)
        shape[axis] *= PLANE
        whole = jnp.zeros(shape, parts[0].dtype)
        for r, part in enumerate(parts):
            whole = lax.dynamic_update_slice_in_dim(whole, part, (self.place ^ r) * size, axis)
        return whole

    def core_sum(self, part, lines):
        width = part.shape[1]
        if self.cores == 2:
            part = part.reshape(lines, 2, -1, width)
            keep = lax.dynamic_index_in_dim(part, self.core, 1, False)
            give = lax.dynamic_index_in_dim(part, 1 - self.core, 1, False)
            got = lax.ppermute(give, "tensor", [(0, 1), (1, 0)])
            return (keep.astype(f32) + got.astype(f32)).astype(bf16)
        return lax.psum_scatter(
            part.reshape(lines, -1, width), "tensor", scatter_dimension=1, tiled=True
        )


def projected(lay, inputs, proj_basis):
    proj = jnp.dot(inputs.astype(f32), proj_basis, precision=lax.Precision.HIGHEST).astype(bf16)
    proj = lax.all_gather(proj, "tensor", axis=0, tiled=True)
    return [proj] + [lay.across(proj, r) for r in range(1, PLANE)]


def panel_shares(lay, plane_proj, pieces):
    panel = sum(tn(q, a) for q, a in zip(plane_proj, pieces))
    share = panel.shape[0] // lay.line
    share_of = lambda x, s: lax.dynamic_slice_in_dim(x, (lay.level ^ s) * share, share, 0)
    half = panel.astype(bf16)
    return [share_of(panel, 0)] + [lay.levels(share_of(half, s), s) for s in range(1, lay.line)]


def panel_quarter(lay, shares):
    summed = sum(x.astype(f32) for x in shares).astype(bf16)
    share, quarter = summed.shape
    panel_q = jnp.zeros((share * lay.line, quarter), bf16)
    for s in range(lay.line):
        got = lay.levels(summed, s) if s else summed
        panel_q = lax.dynamic_update_slice_in_dim(panel_q, got, (lay.level ^ s) * share, 0)
    return panel_q


def panel_whole(lay, panel_q):
    return lay.in_order([panel_q] + [lay.across(panel_q, r) for r in range(1, PLANE)], 1)


def updated(lay, proj_basis, panel, momentum, tokens):
    rows, rank = momentum.shape[0], proj_basis.shape[1]
    basis_rows = lax.dynamic_slice_in_dim(proj_basis, lay.me * rows, rows, 0)
    scale = math.sqrt(proj_basis.shape[0] / rank) / math.sqrt(tokens)
    update = jnp.dot(basis_rows.astype(bf16), panel, preferred_element_type=f32)
    return momentum_decay * momentum + update * scale


def long_line(inputs, out_grad, weight, proj_basis, momentum):
    lay = Layout()
    line, level, cores = lay.line, lay.level, lay.cores
    tokens = out_grad.shape[0]
    pieces = [lay.cut(out_grad, 0)] + [lay.across(lay.cut(out_grad, r), r) for r in range(1, PLANE)]
    weights = [lay.cut(weight, 0)] + [lay.across(lay.cut(weight, r), r) for r in range(1, PLANE)]
    groups = [[p + PLANE * z for z in range(line)] for p in range(PLANE)]
    shares = panel_shares(lay, projected(lay, inputs, proj_basis), pieces)
    panel = panel_whole(lay, panel_quarter(lay, shares))
    new_momentum = updated(lay, proj_basis, panel, momentum, tokens * lay.replicas)
    held = lay.in_order(weights, 0)
    width = held.shape[0]
    total = 0.0
    for r, piece in enumerate(pieces):
        block = lax.all_gather(piece, "dp", axis_index_groups=groups, axis=0, tiled=True)
        part = lay.core_sum(nt(block, held).astype(bf16), line)
        total = total + (lay.across(part, r) if r else part).astype(f32)
    total = total.astype(bf16)
    input_grad = jnp.zeros((tokens // cores, line * width), bf16)
    for s in range(line):
        got = lax.dynamic_index_in_dim(total, level ^ s, 0, False)
        got = lay.levels(got, s) if s else got
        input_grad = lax.dynamic_update_slice_in_dim(input_grad, got, (level ^ s) * width, 1)
    return input_grad, new_momentum


def products(lay, sources, buffers, fills, jobs, width):
    scalars = jnp.stack([lay.place, lay.core]).astype(jnp.int32)
    block = buffers[jobs[0][0]][0]
    half = block // PLANE // 2
    piece = width // PLANE

    def kernel(scalar_ref, *refs):
        ins, refs = refs[: len(sources)], refs[len(sources):]
        keep_ref, give_ref, *scratch = refs
        buffer_refs, sems = scratch[:-1], scratch[-1]
        place, core = scalar_ref[0], scalar_ref[1]
        copies = []
        for i, (s, c0, b, r0, c1, cols) in enumerate(fills):
            n = sources[s].shape[0]
            copies.append(
                pltpu.make_async_copy(
                    ins[s].at[:, pl.ds(c0, cols)],
                    buffer_refs[b].at[pl.ds(r0, n), pl.ds(c1, cols)],
                    sems.at[i],
                )
            )
        for copy in copies:
            copy.start()
        waited = set()

        def need(ids):
            for i in ids:
                if i not in waited:
                    copies[i].wait()
                    waited.add(i)

        for at, (a, b, a0, b0, cols, a_ids, b_ids) in enumerate(jobs):
            need(a_ids)
            for r in range(PLANE):
                need(b_ids(r))
                column = at * width + pl.multiple_of((place ^ r) * piece, piece)
                for p in range(0, PLANE, 2):
                    x = nt(
                        buffer_refs[a][2 * p * half:(2 * p + 4) * half, a0:a0 + cols],
                        buffer_refs[b][r * piece:(r + 1) * piece, b0:b0 + cols],
                    ).astype(bf16)
                    for i in range(2):
                        low, high = x[2 * i * half:][:half], x[(2 * i + 1) * half:][:half]
                        keep_ref[p + i, :, pl.ds(column, piece)] = jnp.where(core == 0, low, high)
                        give_ref[p + i, :, pl.ds(column, piece)] = jnp.where(core == 0, high, low)
        need(range(len(copies)))

    out = jax.ShapeDtypeStruct((PLANE, half, len(jobs) * width), bf16)
    return pl.pallas_call(
        kernel,
        out_shape=(out, out),
        in_specs=[pl.BlockSpec(memory_space=pltpu.SMEM)]
        + [pl.BlockSpec(memory_space=pl.ANY)] * len(sources),
        out_specs=[pl.BlockSpec(memory_space=pltpu.VMEM)] * 2,
        scratch_shapes=[pltpu.VMEM(shape, bf16) for shape in buffers]
        + [pltpu.SemaphoreType.DMA((len(fills),))],
        compiler_params=pltpu.CompilerParams(vmem_limit_bytes=36 * 2**20),
        cost_estimate=pl.CostEstimate(flops=10**6, bytes_accessed=10**5, transcendentals=0),
    )(scalars, *sources)


def line_of_four(inputs, out_grad, weight, proj_basis, momentum):
    lay = Layout()
    level, across = lay.level, lay.across
    inner = (level == 1) | (level == 2)
    tokens, hidden = out_grad.shape
    rows = weight.shape[0]
    width, block = rows * PLANE, tokens * PLANE
    both = hidden // PLANE
    half = both // 2
    low, high = slice(0, half), slice(half, both)
    end_swap = lambda x: lay.levels(x, 1)
    mid_swap = lambda x: lay.levels(x, 3, (1, 2))
    swap = lambda x: lax.ppermute(x, "tensor", [(0, 1), (1, 0)])
    send = lambda a, w: jnp.where(inner, a, w)

    cuts = [lay.cut(out_grad, r) for r in range(PLANE)]
    plane = [across(cuts[r], r) for r in (1, 2)]
    e0, m0 = end_swap(cuts[0]), mid_swap(cuts[0])
    plane.append(across(after(cuts[3], *plane), 3))
    weight = after(weight, e0, m0)
    parts = [lay.cut(weight, r) for r in range(PLANE)]
    sides = after(jnp.concatenate(plane[:2], 0), e0, m0)
    e1, m1 = end_swap(sides), mid_swap(sides)
    e2, m2 = end_swap(plane[2]), mid_swap(plane[2])
    parts[1:3] = [across(after(parts[r], *plane), r) for r in (1, 2)]
    parts[3] = across(after(parts[3], *parts[1:3]), 3)
    joined = lambda x, c: jnp.concatenate([y[:, c] for y in x], 0)
    near_e, near_m = [e0, after(e1, m2), e2], [m0, m1, m2]
    e_high = joined(near_e, high)
    m_low = joined(near_m, low)
    far0 = mid_swap(joined(near_e, low))
    got_a = send(m_low, jnp.concatenate([w[:, high] for w in parts[:2]], 0))
    got_a = end_swap(got_a)
    proj = projected(lay, after(inputs, e1, m1), proj_basis)
    far1, got = [], []
    for i, w in enumerate(parts[2:]):
        rows_i = slice(i * 2 * tokens, (i + 1) * 2 * tokens)
        far1.append(mid_swap(after(e_high[rows_i], far0, got_a)))
        got.append(end_swap(after(send(far0[rows_i], w[:, high]), got_a, parts[3], *proj)))

    weight_fills = lambda first, b: [(first + r, 0, b, r * rows, 0, both) for r in range(PLANE)]
    none = lambda r: ()
    early0 = send(m_low, got_a)
    own = [after(cuts[0], far0), sides, plane[2]]
    sources = [*own, *near_e, early0, *near_m, *parts]
    starts = (0, tokens, 3 * tokens)
    fills = [(i, 0, 0, row, 0, both) for i, row in enumerate(starts)] + weight_fills(10, 3)
    fills += [(3 + i, 0, 1, row, 0, both) for i, row in enumerate(starts)]
    fills += [(6, 0, 2, 0, 0, half)]
    fills += [(7 + i, half, 2, row, half, half) for i, row in enumerate(starts)]
    jobs = [
        (0, 3, 0, 0, both, (0, 1, 2), lambda r: (3 + r,)),
        (1, 3, 0, 0, both, (7, 8, 9), none),
        (2, 3, 0, 0, both, (10, 11, 12, 13), none),
    ]
    keep, give = products(lay, sources, [(block, both)] * 3 + [(width, both)], fills, jobs, width)
    give = after(give, far1[0], got[0])
    first = (keep.astype(f32) + swap(give).astype(f32)).astype(bf16)
    first_x, first_y = across(first[1], 1), across(first[2], 2)

    panel = sum(tn(q, a) for q, a in zip(proj, [after(cuts[0], give), *plane]))

    late0 = send(far0, jnp.concatenate(got, 0))
    sources = [after(late0, first), *far1, *near_m, *parts, got_a, *got]
    fills = [(0, 0, 0, 0, 0, half)]
    fills += [(1 + i, 0, 0, 2 * i * tokens, half, half) for i in range(2)] + weight_fills(6, 2)
    fills += [(3 + i, half, 1, row, 0, half) for i, row in enumerate(starts)]
    fills += [(10, 0, 3, 0, 0, half), (11, 0, 3, 2 * rows, 0, half), (12, 0, 3, 3 * rows, 0, half)]
    jobs = [
        (0, 2, 0, 0, both, (0, 1, 2), lambda r: (3 + r,)),
        (1, 3, 0, 0, half, (7, 8, 9), lambda r: ((10,), (), (11,), (12,))[r]),
        (0, 3, half, 0, half, (), none),
    ]
    buffers = [(block, both), (block, half), (width, both), (width, half)]
    keep, give = products(lay, sources, buffers, fills, jobs, width)

    def plane_sum(own, *others):
        return sum(x.astype(f32) for x in (own, *others)).astype(bf16)

    first = plane_sum(first[0], first_x, first_y, across(first[3], 3))
    give = after(give, first)
    second = (keep.astype(f32) + swap(give).astype(f32)).astype(bf16)
    arrived = [across(second[r], r) for r in range(1, PLANE)]
    totals = plane_sum(second[0], *arrived)
    part = panel.astype(bf16)
    panel = panel + sum(lay.levels(part, s).astype(f32) for s in range(1, lay.line))
    panel = panel.astype(bf16)
    y1 = after(first[:, width:2 * width], panel)
    panel = after(panel, totals)
    panel = jnp.stack([panel] + [across(panel, r) for r in range(1, PLANE)])
    panel = jnp.concatenate(
        [lax.dynamic_index_in_dim(panel, lay.place ^ p, 0, False) for p in range(PLANE)], 1
    )
    new_momentum = updated(lay, proj_basis, panel, momentum, tokens * lay.replicas)
    y0, early = first[:, :width], first[:, 2 * width:]
    second = totals
    late, early_other, late_other = [second[:, i * width:(i + 1) * width] for i in range(3)]

    z1 = end_swap(y1)
    z3 = mid_swap(early)
    z2 = lay.levels(early, 2, (0, 3))
    late, early_other = after((late, early_other), z2, z3)
    z2b = mid_swap(early_other)
    z_late = lay.levels(jnp.concatenate([late, late_other], 1), 2, (1, 2))
    z3b = lay.levels(late, 3, (0, 3))
    add = lambda *xs: sum(x.astype(f32) for x in xs).astype(bf16)
    z2 = add(z2, z2b, z_late[:, :width])
    z3 = add(z3, z3b, z_late[:, width:])
    input_grad = jnp.concatenate(
        [
            jnp.where(
                level == b,
                y0,
                jnp.where(level == b ^ 1, z1, jnp.where(level == b ^ 2, z2, z3)),
            )
            for b in range(lay.line)
        ],
        1,
    )
    return input_grad, new_momentum


def solution(mesh):
    placed = (
        P(("dp", "tensor"), None),
        P("dp", "tensor"),
        P("dp", "tensor"),
        P(),
        P("dp", "tensor"),
    )
    four = mesh.shape["dp"] == 4 * PLANE and mesh.shape["tensor"] == 2
    return jax.shard_map(
        line_of_four if four else long_line,
        mesh=mesh,
        in_specs=placed,
        out_specs=(P(("dp", "tensor"), None), P("dp", "tensor")),
        check_vma=False,
    )
```

```python
import math

import jax
import jax.numpy as jnp
from jax import lax
from jax.experimental import pallas as pl
from jax.experimental.pallas import tpu as pltpu
from jax.sharding import PartitionSpec as P

momentum_decay = 0.9
PLANE = 4
f32, bf16 = jnp.float32, jnp.bfloat16


def after(x, *first):
    return lax.optimization_barrier((x, first))[0]


def nt(a, b):
    return lax.dot_general(a, b, (((1,), (1,)), ((), ())), preferred_element_type=f32)


def tn(a, b):
    return lax.dot_general(a, b, (((0,), (0,)), ((), ())), preferred_element_type=f32)


class Layout:
    def __init__(self):
        self.replicas, self.cores = lax.axis_size("dp"), lax.axis_size("tensor")
        self.line = self.replicas // PLANE
        self.me, self.core = lax.axis_index("dp"), lax.axis_index("tensor")
        self.place, self.level = self.me % PLANE, self.me // PLANE

    def across(self, x, r):
        return lax.ppermute(x, "dp", [(d, d ^ r) for d in range(self.replicas)])

    def levels(self, x, s, only=None):
        pairs = [
            (d, d ^ (s * PLANE)) for d in range(self.replicas) if only is None or d // PLANE in only
        ]
        return lax.ppermute(x, "dp", pairs)

    def cut(self, x, r):
        quarter = x.shape[1] // PLANE
        return lax.dynamic_slice_in_dim(x, (self.place ^ r) * quarter, quarter, 1)

    def in_order(self, parts, axis):
        size = parts[0].shape[axis]
        shape = list(parts[0].shape)
        shape[axis] *= PLANE
        whole = jnp.zeros(shape, parts[0].dtype)
        for r, part in enumerate(parts):
            whole = lax.dynamic_update_slice_in_dim(whole, part, (self.place ^ r) * size, axis)
        return whole

    def core_sum(self, part, lines):
        width = part.shape[1]
        if self.cores == 2:
            part = part.reshape(lines, 2, -1, width)
            keep = lax.dynamic_index_in_dim(part, self.core, 1, False)
            give = lax.dynamic_index_in_dim(part, 1 - self.core, 1, False)
            got = lax.ppermute(give, "tensor", [(0, 1), (1, 0)])
            return (keep.astype(f32) + got.astype(f32)).astype(bf16)
        return lax.psum_scatter(
            part.reshape(lines, -1, width), "tensor", scatter_dimension=1, tiled=True
        )


def projected(lay, inputs, proj_basis):
    proj = jnp.dot(inputs.astype(f32), proj_basis, precision=lax.Precision.HIGHEST).astype(bf16)
    proj = lax.all_gather(proj, "tensor", axis=0, tiled=True)
    return [proj] + [lay.across(proj, r) for r in range(1, PLANE)]


def panel_shares(lay, plane_proj, pieces):
    panel = sum(tn(q, a) for q, a in zip(plane_proj, pieces))
    share = panel.shape[0] // lay.line
    share_of = lambda x, s: lax.dynamic_slice_in_dim(x, (lay.level ^ s) * share, share, 0)
    half = panel.astype(bf16)
    return [share_of(panel, 0)] + [lay.levels(share_of(half, s), s) for s in range(1, lay.line)]


def panel_quarter(lay, shares):
    summed = sum(x.astype(f32) for x in shares).astype(bf16)
    share, quarter = summed.shape
    panel_q = jnp.zeros((share * lay.line, quarter), bf16)
    for s in range(lay.line):
        got = lay.levels(summed, s) if s else summed
        panel_q = lax.dynamic_update_slice_in_dim(panel_q, got, (lay.level ^ s) * share, 0)
    return panel_q


def panel_whole(lay, panel_q):
    return lay.in_order([panel_q] + [lay.across(panel_q, r) for r in range(1, PLANE)], 1)


def updated(lay, proj_basis, panel, momentum, tokens):
    rows, rank = momentum.shape[0], proj_basis.shape[1]
    basis_rows = lax.dynamic_slice_in_dim(proj_basis, lay.me * rows, rows, 0)
    scale = math.sqrt(proj_basis.shape[0] / rank) / math.sqrt(tokens)
    update = jnp.dot(basis_rows.astype(bf16), panel, preferred_element_type=f32)
    return momentum_decay * momentum + update * scale


def long_line(inputs, out_grad, weight, proj_basis, momentum):
    lay = Layout()
    line, level, cores = lay.line, lay.level, lay.cores
    tokens = out_grad.shape[0]
    pieces = [lay.cut(out_grad, 0)] + [lay.across(lay.cut(out_grad, r), r) for r in range(1, PLANE)]
    weights = [lay.cut(weight, 0)] + [lay.across(lay.cut(weight, r), r) for r in range(1, PLANE)]
    groups = [[p + PLANE * z for z in range(line)] for p in range(PLANE)]
    shares = panel_shares(lay, projected(lay, inputs, proj_basis), pieces)
    panel = panel_whole(lay, panel_quarter(lay, shares))
    new_momentum = updated(lay, proj_basis, panel, momentum, tokens * lay.replicas)
    held = lay.in_order(weights, 0)
    width = held.shape[0]
    total = 0.0
    for r, piece in enumerate(pieces):
        block = lax.all_gather(piece, "dp", axis_index_groups=groups, axis=0, tiled=True)
        part = lay.core_sum(nt(block, held).astype(bf16), line)
        total = total + (lay.across(part, r) if r else part).astype(f32)
    total = total.astype(bf16)
    input_grad = jnp.zeros((tokens // cores, line * width), bf16)
    for s in range(line):
        got = lax.dynamic_index_in_dim(total, level ^ s, 0, False)
        got = lay.levels(got, s) if s else got
        input_grad = lax.dynamic_update_slice_in_dim(input_grad, got, (level ^ s) * width, 1)
    return input_grad, new_momentum


def products(lay, sources, buffers, fills, jobs, width):
    scalars = jnp.stack([lay.place, lay.core]).astype(jnp.int32)
    block = buffers[jobs[0][0]][0]
    half = block // PLANE // 2
    piece = width // PLANE

    def kernel(scalar_ref, *refs):
        ins, refs = refs[: len(sources)], refs[len(sources):]
        keep_ref, give_ref, *scratch = refs
        buffer_refs, sems = scratch[:-1], scratch[-1]
        place, core = scalar_ref[0], scalar_ref[1]
        copies = []
        for i, (s, c0, b, r0, c1, cols) in enumerate(fills):
            n = sources[s].shape[0]
            copies.append(
                pltpu.make_async_copy(
                    ins[s].at[:, pl.ds(c0, cols)],
                    buffer_refs[b].at[pl.ds(r0, n), pl.ds(c1, cols)],
                    sems.at[i],
                )
            )
        for copy in copies:
            copy.start()
        waited = set()

        def need(ids):
            for i in ids:
                if i not in waited:
                    copies[i].wait()
                    waited.add(i)

        for at, (a, b, a0, b0, cols, a_ids, b_ids) in enumerate(jobs):
            need(a_ids)
            for r in range(PLANE):
                need(b_ids(r))
                column = at * width + pl.multiple_of((place ^ r) * piece, piece)
                for p in range(0, PLANE, 2):
                    x = nt(
                        buffer_refs[a][2 * p * half:(2 * p + 4) * half, a0:a0 + cols],
                        buffer_refs[b][r * piece:(r + 1) * piece, b0:b0 + cols],
                    ).astype(bf16)
                    for i in range(2):
                        low, high = x[2 * i * half:][:half], x[(2 * i + 1) * half:][:half]
                        keep_ref[p + i, :, pl.ds(column, piece)] = jnp.where(core == 0, low, high)
                        give_ref[p + i, :, pl.ds(column, piece)] = jnp.where(core == 0, high, low)
        need(range(len(copies)))

    out = jax.ShapeDtypeStruct((PLANE, half, len(jobs) * width), bf16)
    return pl.pallas_call(
        kernel,
        out_shape=(out, out),
        in_specs=[pl.BlockSpec(memory_space=pltpu.SMEM)]
        + [pl.BlockSpec(memory_space=pl.ANY)] * len(sources),
        out_specs=[pl.BlockSpec(memory_space=pltpu.VMEM)] * 2,
        scratch_shapes=[pltpu.VMEM(shape, bf16) for shape in buffers]
        + [pltpu.SemaphoreType.DMA((len(fills),))],
        compiler_params=pltpu.CompilerParams(vmem_limit_bytes=36 * 2**20),
        cost_estimate=pl.CostEstimate(flops=10**6, bytes_accessed=10**5, transcendentals=0),
    )(scalars, *sources)


def line_of_four(inputs, out_grad, weight, proj_basis, momentum):
    lay = Layout()
    level, across = lay.level, lay.across
    inner = (level == 1) | (level == 2)
    tokens, hidden = out_grad.shape
    rows = weight.shape[0]
    width, block = rows * PLANE, tokens * PLANE
    both = hidden // PLANE
    half = both // 2
    low, high = slice(0, half), slice(half, both)
    end_swap = lambda x: lay.levels(x, 1)
    mid_swap = lambda x: lay.levels(x, 3, (1, 2))
    swap = lambda x: lax.ppermute(x, "tensor", [(0, 1), (1, 0)])
    send = lambda a, w: jnp.where(inner, a, w)

    cuts = [lay.cut(out_grad, r) for r in range(PLANE)]
    plane = [across(cuts[r], r) for r in (1, 2)]
    e0, m0 = end_swap(cuts[0]), mid_swap(cuts[0])
    plane.append(across(after(cuts[3], *plane), 3))
    weight = after(weight, e0, m0)
    parts = [lay.cut(weight, r) for r in range(PLANE)]
    sides = after(jnp.concatenate(plane[:2], 0), e0, m0)
    e1, m1 = end_swap(sides), mid_swap(sides)
    e2, m2 = end_swap(plane[2]), mid_swap(plane[2])
    parts[1:3] = [across(after(parts[r], *plane), r) for r in (1, 2)]
    parts[3] = across(after(parts[3], *parts[1:3]), 3)
    joined = lambda x, c: jnp.concatenate([y[:, c] for y in x], 0)
    near_e, near_m = [e0, after(e1, m1, m2), e2], [m0, m1, m2]
    e_high = joined(near_e, high)
    m_low = joined(near_m, low)
    far0 = mid_swap(joined(near_e, low))
    got_a = send(m_low, jnp.concatenate([w[:, high] for w in parts[:2]], 0))
    got_a = end_swap(got_a)
    proj = projected(lay, after(inputs, e1, m1), proj_basis)
    far1, got = [], []
    for i, w in enumerate(parts[2:]):
        rows_i = slice(i * 2 * tokens, (i + 1) * 2 * tokens)
        far1.append(mid_swap(after(e_high[rows_i], far0, got_a)))
        got.append(end_swap(after(send(far0[rows_i], w[:, high]), got_a, parts[3], *proj)))

    weight_fills = lambda first, b: [(first + r, 0, b, r * rows, 0, both) for r in range(PLANE)]
    none = lambda r: ()
    early0 = send(m_low, got_a)
    own = [after(cuts[0], far0), sides, plane[2]]
    sources = [*own, *near_e, early0, *near_m, *parts]
    starts = (0, tokens, 3 * tokens)
    fills = [(i, 0, 0, row, 0, both) for i, row in enumerate(starts)] + weight_fills(10, 3)
    fills += [(3 + i, 0, 1, row, 0, both) for i, row in enumerate(starts)]
    fills += [(6, 0, 2, 0, 0, half)]
    fills += [(7 + i, half, 2, row, half, half) for i, row in enumerate(starts)]
    jobs = [
        (0, 3, 0, 0, both, (0, 1, 2), lambda r: (3 + r,)),
        (1, 3, 0, 0, both, (7, 8, 9), none),
        (2, 3, 0, 0, both, (10, 11, 12, 13), none),
    ]
    keep, give = products(lay, sources, [(block, both)] * 3 + [(width, both)], fills, jobs, width)
    give = after(give, far1[0], got[0])
    first = (keep.astype(f32) + swap(give).astype(f32)).astype(bf16)
    first_x, first_y = across(first[1], 1), across(first[2], 2)

    panel = sum(tn(q, a) for q, a in zip(proj, [after(cuts[0], give), *plane]))

    late0 = send(far0, jnp.concatenate(got, 0))
    sources = [after(late0, first), *far1, *near_m, *parts, got_a, *got]
    fills = [(0, 0, 0, 0, 0, half)]
    fills += [(1 + i, 0, 0, 2 * i * tokens, half, half) for i in range(2)] + weight_fills(6, 2)
    fills += [(3 + i, half, 1, row, 0, half) for i, row in enumerate(starts)]
    fills += [(10, 0, 3, 0, 0, half), (11, 0, 3, 2 * rows, 0, half), (12, 0, 3, 3 * rows, 0, half)]
    jobs = [
        (0, 2, 0, 0, both, (0, 1, 2), lambda r: (3 + r,)),
        (1, 3, 0, 0, half, (7, 8, 9), lambda r: ((10,), (), (11,), (12,))[r]),
        (0, 3, half, 0, half, (), none),
    ]
    buffers = [(block, both), (block, half), (width, both), (width, half)]
    keep, give = products(lay, sources, buffers, fills, jobs, width)

    def plane_sum(own, *others):
        return sum(x.astype(f32) for x in (own, *others)).astype(bf16)

    first = plane_sum(first[0], first_x, first_y, across(first[3], 3))
    give = after(give, first)
    second = (keep.astype(f32) + swap(give).astype(f32)).astype(bf16)
    arrived = [across(second[r], r) for r in range(1, PLANE)]
    totals = plane_sum(second[0], *arrived)
    part = panel.astype(bf16)
    panel = panel + sum(lay.levels(part, s).astype(f32) for s in range(1, lay.line))
    panel = panel.astype(bf16)
    y1 = after(first[:, width:2 * width], panel)
    panel = after(panel, totals)
    panel = jnp.stack([panel] + [across(panel, r) for r in range(1, PLANE)])
    panel = jnp.concatenate(
        [lax.dynamic_index_in_dim(panel, lay.place ^ p, 0, False) for p in range(PLANE)], 1
    )
    new_momentum = updated(lay, proj_basis, panel, momentum, tokens * lay.replicas)
    y0, early = first[:, :width], first[:, 2 * width:]
    second = totals
    late, early_other, late_other = [second[:, i * width:(i + 1) * width] for i in range(3)]

    z1 = end_swap(y1)
    z3 = mid_swap(early)
    z2 = lay.levels(early, 2, (0, 3))
    late, early_other = after((late, early_other), z2, z3)
    z2b = mid_swap(early_other)
    z_late = lay.levels(jnp.concatenate([late, late_other], 1), 2, (1, 2))
    z3b = lay.levels(late, 3, (0, 3))
    add = lambda *xs: sum(x.astype(f32) for x in xs).astype(bf16)
    z2 = add(z2, z2b, z_late[:, :width])
    z3 = add(z3, z3b, z_late[:, width:])
    input_grad = jnp.concatenate(
        [
            jnp.where(
                level == b,
                y0,
                jnp.where(level == b ^ 1, z1, jnp.where(level == b ^ 2, z2, z3)),
            )
            for b in range(lay.line)
        ],
        1,
    )
    return input_grad, new_momentum


def solution(mesh):
    placed = (
        P(("dp", "tensor"), None),
        P("dp", "tensor"),
        P("dp", "tensor"),
        P(),
        P("dp", "tensor"),
    )
    four = mesh.shape["dp"] == 4 * PLANE and mesh.shape["tensor"] == 2
    return jax.shard_map(
        line_of_four if four else long_line,
        mesh=mesh,
        in_specs=placed,
        out_specs=(P(("dp", "tensor"), None), P("dp", "tensor")),
        check_vma=False,
    )
```
